512 devices in a mesh: expert: 8 (over x, y_hi), dp: 64 (over z, y_lo, core).
Axes of the slice: x: 4, y: 8 (y_hi: 2, y_lo: 4; y = y_hi * 4 + y_lo), z: 8, core: 2. Of those that a mesh axis runs over, the one named last changes fastest.
Arguments:
- tokens: bfloat16 [64, 16, 2048], P('dp', 'expert'), may hold values from -6 to 6
- out_grad: bfloat16 [64, 16, 2048], P('dp', 'expert'), may hold values from -6 to 6
- expert_ids: int32 [64, 16, 2], P('dp'), may hold values from 0 to 7, as said below
- gate_scores: bfloat16 [64, 16, 2], P('dp'), may hold values from 0.25 to 1
- w_gate: bfloat16 [8, 2048, 8192], P('expert', None, 'dp'), may hold values from -0.125 to 0.125
- w_up: bfloat16 [8, 2048, 8192], P('expert', None, 'dp'), may hold values from -0.125 to 0.125
- w_down: bfloat16 [8, 8192, 2048], P('expert', 'dp'), may hold values from -0.0625 to 0.0625
Outputs:
- token_grad: bfloat16 [64, 16, 2048], P('dp', 'expert')
- grad_gate: bfloat16 [8, 2048, 8192], P('expert', None, 'dp')
- grad_up: bfloat16 [8, 2048, 8192], P('expert', None, 'dp')
- grad_down: bfloat16 [8, 8192, 2048], P('expert', 'dp')
The draws below stay inside these ranges and needn't reach their ends.
Inputs may be any that keep to these rules, and one draw needn't show every extreme that they name: `expert_ids`: each token names two different experts; within a group no expert is named by more than 7 tokens, and in every group some expert is named by exactly 7 tokens.
All inputs are finite; a program needn't handle non-finite values.
Results may differ from the reference program's by a relative error of at most 0.0058.
Values may be sent and summed in bfloat16 or wider, within the bound.
A program may use at most 64 MiB of HBM per device.

```python
import jax
import jax.numpy as jnp
from jax import lax

D = 2048
FF = 8192
EXPERTS = 8
GROUPS = 64
GROUP_TOK = 16
CAP = 7


def draw_expert_ids(key, part):
    base = jax.random.fold_in(key, 11)
    lead_key, score_key = jax.random.split(base, 2)
    leader = jax.random.randint(lead_key, (GROUPS,), 0, EXPERTS)
    noise = jax.random.randint(score_key, (GROUP_TOK, GROUPS, EXPERTS), 0, 64)
    expert_range = jnp.arange(EXPERTS, dtype=jnp.int32)

    def assign(loads, noise_row):
        score = noise_row + jnp.where(expert_range[None, :] == leader[:, None], 4096, 0)
        score = jnp.where(loads >= CAP, -100000, score)
        score = score * 16 + expert_range[None, :]
        picked = jnp.argsort(-score, axis=-1, stable=True)[:, :2].astype(jnp.int32)
        onehot = (picked[:, :, None] == expert_range[None, None, :]).astype(jnp.int32)
        return (loads + jnp.sum(onehot, axis=1), picked)
    start_loads = jnp.zeros((GROUPS, EXPERTS), jnp.int32)
    final_loads, picks = lax.scan(assign, start_loads, noise)
    return jnp.transpose(picks, (1, 0, 2))


def block_levels(key, shape, shards, smallest, largest):
    loudness = 1.0
    for position, shards_of in shards:
        steps = jax.random.uniform(jax.random.fold_in(jax.random.fold_in(key, 6), position), (shards_of,), jnp.float32, smallest / len(shards), largest / len(shards))
        loudness = loudness * jnp.repeat(jnp.exp(steps), shape[position] // shards_of).reshape((-1,) + (1,) * (len(shape) - 1 - position))
    return loudness


def bell_draw(own_key, dims, deviation, reach, shards=(), kind=jnp.bfloat16):
    array = jax.random.normal(own_key, dims, jnp.float32) * deviation
    if len(shards) > 0:
        array = block_levels(own_key, dims, shards, -0.22, 0.18) * array
    return jnp.clip(array, min=-reach, max=reach).astype(kind)


def setup_inputs(seed: int = 0) -> dict:
    seeds = jax.random.split(jax.random.key(seed), 8)
    tokens = bell_draw(seeds[0], (GROUPS, GROUP_TOK, D), 1.0, 6.0, ((0, 64), (1, 8)))
    out_grad = bell_draw(seeds[1], (GROUPS, GROUP_TOK, D), 1.0, 6.0, ((0, 64), (1, 8)))
    expert_ids = draw_expert_ids(jax.random.fold_in(seeds[7], 71), 0)
    gate_scores = jnp.clip(0.25 + 0.75 * jax.random.uniform(seeds[3], (GROUPS, GROUP_TOK, 2), jnp.float32) ** block_levels(seeds[3], (GROUPS, GROUP_TOK, 2), ((0, 64),), -0.2, 0.2), 0.25, 1.0).astype(jnp.bfloat16)
    w_gate = bell_draw(seeds[4], (EXPERTS, D, FF), D ** -0.5, 0.125, ((0, 8), (2, 64)))
    w_up = bell_draw(seeds[5], (EXPERTS, D, FF), D ** -0.5, 0.125, ((0, 8), (2, 64)))
    w_down = bell_draw(seeds[6], (EXPERTS, FF, D), FF ** -0.5, 0.0625, ((0, 8), (1, 64)))
    return dict(tokens=tokens, out_grad=out_grad, expert_ids=expert_ids, gate_scores=gate_scores, w_gate=w_gate, w_up=w_up, w_down=w_down)


def expert_pass(operands):
    input_rows, grad_rows, gate_mat, up_mat, down_mat = operands
    pre_gate = jnp.dot(input_rows, gate_mat, preferred_element_type=jnp.float32)
    pre_up = jnp.dot(input_rows, up_mat, preferred_element_type=jnp.float32)
    sigmoid_gate = jax.nn.sigmoid(pre_gate)
    activated = pre_gate * sigmoid_gate
    hidden = (activated * pre_up).astype(jnp.bfloat16)
    grad_down = jnp.dot(hidden.T, grad_rows, preferred_element_type=jnp.float32).astype(jnp.bfloat16)
    grad_hidden = jnp.dot(grad_rows, down_mat.T, preferred_element_type=jnp.float32)
    gate_delta = (grad_hidden * pre_up * sigmoid_gate * (1.0 + pre_gate * (1.0 - sigmoid_gate))).astype(jnp.bfloat16)
    up_delta = (grad_hidden * activated).astype(jnp.bfloat16)
    grad_gate = jnp.dot(input_rows.T, gate_delta, preferred_element_type=jnp.float32).astype(jnp.bfloat16)
    grad_up = jnp.dot(input_rows.T, up_delta, preferred_element_type=jnp.float32).astype(jnp.bfloat16)
    row_grad = jnp.dot(gate_delta, gate_mat.T, preferred_element_type=jnp.float32)
    row_grad = row_grad + jnp.dot(up_delta, up_mat.T, preferred_element_type=jnp.float32)
    return grad_gate, grad_up, grad_down, row_grad


def slot_table(expert_ids, experts):
    expert_range = jnp.arange(experts, dtype=jnp.int32)
    naming = jnp.sum((expert_ids[..., :, None] == expert_range).astype(jnp.int32), axis=-2).astype(jnp.int32)
    before = (jnp.cumsum(naming, axis=-2).astype(jnp.int32) - naming).astype(jnp.int32)
    return jnp.take_along_axis(before, expert_ids, axis=-1).astype(jnp.int32)


def reference(tokens, out_grad, expert_ids, gate_scores, w_gate, w_up, w_down):
    groups, group_tok, width = tokens.shape
    experts = w_gate.shape[0]
    slot_ids = slot_table(expert_ids, experts)
    expert_range = jnp.arange(experts, dtype=jnp.int32)
    slot_range = jnp.arange(CAP, dtype=jnp.int32)
    matches = (expert_ids[:, None, None, :, :] == expert_range[None, :, None, None, None]) & (slot_ids[:, None, None, :, :] == slot_range[None, None, :, None, None])
    placing = jnp.sum(matches.astype(jnp.float32), axis=-1)
    weighting = jnp.sum(matches.astype(jnp.float32) * gate_scores.astype(jnp.float32)[:, None, None, :, :], axis=-1)
    input_rows = jnp.einsum("gect,gtd->egcd", placing, tokens.astype(jnp.float32)).astype(jnp.bfloat16)
    grad_rows = jnp.einsum("gect,gtd->egcd", weighting, out_grad.astype(jnp.float32)).astype(jnp.bfloat16)
    input_rows = input_rows.reshape(experts, groups * CAP, width)
    grad_rows = grad_rows.reshape(experts, groups * CAP, width)
    grad_gate, grad_up, grad_down, row_grad = lax.map(expert_pass, (input_rows, grad_rows, w_gate, w_up, w_down))
    row_grad = row_grad.reshape(experts, groups, CAP, width)
    token_grad = jnp.einsum("gect,egcd->gtd", placing, row_grad, precision=lax.Precision.HIGHEST)
    return token_grad.astype(jnp.bfloat16), grad_gate, grad_up, grad_down
```

```python
import jax
import jax.numpy as jnp
from jax import lax
from jax.experimental import pallas as pl
from jax.experimental.pallas import tpu as pltpu
from jax.sharding import PartitionSpec as P

MESH = pl.DeviceIdType.MESH
F32, BF16 = jnp.float32, jnp.bfloat16

NE = 8
NZ = 8
NY = 4
NG = NY * 2
CAP = 7
D = 2048
HD = D // 2
FS = 128
R = NG * CAP
B = 2 * R
CUT = 64
PIECES = ((0, CUT), (CUT, B - CUT))
NT = (((1,), (1,)), ((), ()))


def dot(a, b):
    return jnp.dot(a, b, preferred_element_type=F32)


def dot_nt(a, b):
    return lax.dot_general(a, b, NT, preferred_element_type=F32)


def iota(shape, dim):
    return lax.broadcasted_iota(jnp.int32, shape, dim)


def spread(rows, cols, r_dim):
    r = iota((rows, cols), r_dim)
    c = iota((rows, cols), 1 - r_dim)
    low = jnp.where(r < R, r, r - R)
    group = (low * 37) >> 8
    place = group * 9 + low + jnp.where(r < R, 0, 8)
    return jnp.where(place == c, 1.0, 0.0).astype(BF16)


def kernel(
    tok, cot, ids, scores, wg, wu, wd,
    o_tok, o_gg, o_gu, o_gd,
    gbuf, gf, pick, ybuf, blocks, wall, wdv, wsib, stack, ssib, part, sbuf, rbuf, ysend, yrecv, esend, erecv, gout, gdv,
    load_sem, own_sem, ws_send, ws_recv, g_send, g_recv, y_send, y_recv, sib_send, sib_recv, ag_send, ag_recv,
    ss_send, ss_recv, rs_send, rs_recv, y2_send, y2_recv, e_send, e_recv, out_sem,
):
    e = lax.axis_index("expert")
    d = lax.axis_index("dp")
    z = d // NG
    g = d - z * NG
    h = g % 2
    sib = (e, d + 1 - 2 * h)
    zp = (e, lax.rem(z + 1, NZ) * NG + g)
    zm = (e, lax.rem(z + NZ - 1, NZ) * NG + g)

    def wrap(k):
        return lax.rem(k + 2 * NZ, NZ)

    sent = []

    def send(src, dst, s_sem, r_sem, to):
        copy = pltpu.make_async_remote_copy(
            src_ref=src, dst_ref=dst, send_sem=s_sem, recv_sem=r_sem, device_id=to, device_id_type=MESH
        )
        copy.start()
        sent.append(copy)

    def arrived(dst, r_sem):
        pltpu.make_async_remote_copy(
            src_ref=dst, dst_ref=dst, send_sem=r_sem, recv_sem=r_sem, device_id=sib, device_id_type=MESH
        ).wait_recv()

    loads = [
        pltpu.make_async_copy(tok.at[0], gbuf.at[e, 0], own_sem.at[0]),
        pltpu.make_async_copy(cot.at[0], gbuf.at[e, 1], own_sem.at[1]),
        pltpu.make_async_copy(wd.at[0], wdv, load_sem.at[2]),
        pltpu.make_async_copy(wg.at[0], wall.at[:, 0:FS], load_sem.at[0]),
        pltpu.make_async_copy(wu.at[0], wall.at[:, FS : 2 * FS], load_sem.at[1]),
    ]
    for copy in loads:
        copy.start()

    barrier = pltpu.get_barrier_semaphore()
    for i in range(1, NE):
        pl.semaphore_signal(barrier, inc=1, device_id=(lax.rem(e + i, NE), d), device_id_type=MESH)
    for i in range(1, NG):
        pl.semaphore_signal(barrier, inc=1, device_id=(e, z * NG + lax.rem(g + i, NG)), device_id_type=MESH)
    for to in (zp, zm):
        pl.semaphore_signal(barrier, inc=1, device_id=to, device_id_type=MESH)
    loads[0].wait()
    loads[1].wait()
    pl.semaphore_wait(barrier, NE - 1 + NG - 1 + 2)

    for i in range(1, NE):
        send(gbuf.at[e], gbuf.at[e], g_send.at[i], g_recv.at[e], (lax.rem(e + i, NE), d))
    other = pl.ds(pl.multiple_of((1 - h) * HD, HD), HD)
    send(wg.at[0, other, :], wsib.at[:, 0:FS], ws_send.at[0], ws_recv.at[0], sib)
    send(wu.at[0, other, :], wsib.at[:, FS : 2 * FS], ws_send.at[1], ws_recv.at[1], sib)

    hits = jnp.where(ids[...] == e, 1.0, 0.0)
    named_t = jnp.sum(hits, axis=0, keepdims=True)
    score_t = jnp.sum(hits * scores[...].astype(F32), axis=0, keepdims=True)
    row16, col16 = iota((16, 16), 0), iota((16, 16), 1)
    eye = jnp.where(row16 == col16, 1.0, 0.0)
    named = jnp.sum(eye * named_t, axis=1, keepdims=True)
    slot_t = jnp.sum(jnp.where(row16 < col16, named, 0.0), axis=0, keepdims=True)
    slot = jnp.sum(jnp.where(col16 < row16, named_t, 0.0), axis=1, keepdims=True)
    placing = jnp.where(slot_t == iota((8, 16), 0).astype(F32), named_t, 0.0)
    placing_t = jnp.where(slot == iota((16, 8), 1).astype(F32), named, 0.0)
    weighting = placing * score_t
    zero = jnp.zeros((8, 16), F32)
    picking = jnp.concatenate(
        [jnp.concatenate([placing, zero], axis=1), jnp.concatenate([zero, weighting], axis=1)], axis=0
    ).astype(BF16)

    loads[2].wait()
    wall[:, 2 * FS : 3 * FS] = wdv[...].T

    for i in range(1, NE):
        src = lax.rem(e + i, NE)
        arrived(gbuf.at[src], g_recv.at[src])
    for s in range(NE):
        for a in range(2):
            gf[a * 16 + 2 * s : a * 16 + 2 * s + 2, :] = gbuf[s, a].astype(F32)
    picked = dot(picking, gf[...].astype(BF16)).astype(BF16)
    pick[0] = picked[:, :HD]
    pick[1] = picked[:, HD:]

    for i in range(1, NG):
        to = lax.rem(g + i, NG)
        send(pick.at[to % 2], ybuf.at[g], y_send.at[i], y_recv.at[g], (e, z * NG + to))
    ybuf[g] = pick[h]
    gather = spread(B, NG * 16, 0)
    for i in range(1, NG):
        src = lax.rem(g + i, NG)
        arrived(ybuf.at[src], y_recv.at[src])
    blocks[z, h] = dot(gather, ybuf[...].reshape(NG * 16, HD)).astype(BF16)

    def piece(p):
        return pl.ds(*PIECES[p])

    def ag_start(way, step, p, k):
        ref = blocks.at[k, h, piece(p)]
        send(ref, ref, ag_send.at[way, step, p], ag_recv.at[way, step, p], (zp, zm)[way])

    def ag_wait(way, step, p, k):
        arrived(blocks.at[k, h, piece(p)], ag_recv.at[way, step, p])

    def to_sibling(k):
        ref = blocks.at[k, h]
        send(ref, ref, sib_send.at[k], sib_recv.at[k], sib)

    def fwd(k):
        arrived(blocks.at[k, 1 - h], sib_recv.at[k])
        r = dot(blocks[k, 0], wall[:HD, :]) + dot(blocks[k, 1], wall[HD:, :])
        gate, up, gh = r[:R, :FS], r[:R, FS : 2 * FS], r[R:, 2 * FS :]
        sig = jax.nn.sigmoid(gate)
        act = gate * sig
        none = jnp.zeros((R, FS), F32)
        gate_delta = gh * up * sig * (1.0 + gate * (1.0 - sig))
        stack[k, :, 0:FS] = jnp.concatenate([gate_delta, none], axis=0).astype(BF16)
        stack[k, :, FS : 2 * FS] = jnp.concatenate([gh * act, none], axis=0).astype(BF16)
        stack[k, :, 2 * FS :] = jnp.concatenate([none, act * up], axis=0).astype(BF16)
        send(stack.at[k, 0:CUT, 0 : 2 * FS], ssib.at[k], ss_send.at[k], ss_recv.at[k], sib)

    mine = pl.ds(pl.multiple_of(h * HD, HD), HD)

    def row_grad(k):
        arrived(ssib.at[k], ss_recv.at[k])
        r = dot_nt(stack[k, 0:CUT, 0 : 2 * FS], wall[mine, 0 : 2 * FS]) + dot_nt(ssib[k], wsib[...])
        part[k] = jnp.concatenate([r[:R, : HD // 2], r[:R, HD // 2 :]], axis=0)

    for p in range(2):
        for way in range(2):
            ag_start(way, 0, p, z)
    to_sibling(z)
    for copy in loads[3:]:
        copy.wait()
    for i in range(2):
        arrived(wsib.at[:, i * FS : (i + 1) * FS], ws_recv.at[i])

    def near(way, s):
        return wrap(z - s if way == 0 else z + s)

    def rs_start(way, step, p, value):
        rows = PIECES[p]
        sbuf[way, step, rows[0] : rows[0] + rows[1]] = value.astype(BF16)
        send(
            sbuf.at[way, step, piece(p)], rbuf.at[way, step, piece(p)],
            rs_send.at[way, step, p], rs_recv.at[way, step, p], (zp, zm)[way],
        )

    def rs_take(way, step, p):
        arrived(rbuf.at[way, step, piece(p)], rs_recv.at[way, step, p])
        rows = PIECES[p]
        return rbuf[way, step, rows[0] : rows[0] + rows[1]].astype(F32)

    def part_of(k, p):
        rows = PIECES[p]
        return part[k, rows[0] : rows[0] + rows[1]]

    work = {
        (1, 0): [(fwd, z)],
        (1, 1): [],
        (2, 0): [(fwd, near(0, 1)), (row_grad, z)],
        (2, 1): [(fwd, near(1, 1))],
        (3, 0): [(fwd, near(0, 2)), (row_grad, near(0, 1))],
        (3, 1): [(fwd, near(1, 2)), (row_grad, near(1, 1))],
    }
    for s in range(1, 4):
        for p in range(2):
            for way in range(2):
                ag_wait(way, s - 1, p, near(way, s))
                if s < 3 or p == way:
                    ag_start(way, s, p, near(way, s))
            if p == 1:
                for way in range(2):
                    to_sibling(near(way, s))
            for f, k in work[s, p]:
                f(k)
    far = wrap(z + 4)
    fwd(near(0, 3))
    row_grad(near(0, 2))
    fwd(near(1, 3))
    row_grad(near(1, 2))
    for way in range(2):
        ag_wait(way, 3, way, far)
    to_sibling(far)
    for way in range(2):
        row_grad(near(way, 3))
    for way in range(2):
        rs_start(way, 1, 1 - way, part_of(near(1 - way, 3), 1 - way))
    fwd(far)
    row_grad(far)
    for way in range(2):
        rs_start(way, 0, way, part_of(far, way))

    stack_t = stack[...].reshape(NZ * B, 3 * FS).T

    def weight_grad(n):
        width = D // 4
        at = n % 2 * width
        cols = blocks[:, n // 2, :, at : at + width].reshape(NZ * B, width)
        r = dot(stack_t, cols)
        gdv[:, n * width : (n + 1) * width] = r[2 * FS :].astype(BF16)
        gout[n * width : (n + 1) * width, :] = r[: 2 * FS].T.astype(BF16)

    for j in range(1, 4):
        weight_grad(j - 1)
        for p in range(2):
            for way in range(2):
                if j == 1 and p != way:
                    continue
                rs_start(way, j, p, part_of(near(1 - way, 4 - j), p) + rs_take(way, j - 1, p))
    weight_grad(3)
    outs = [
        pltpu.make_async_copy(gout.at[:, 0:FS], o_gg.at[0], out_sem.at[0]),
        pltpu.make_async_copy(gout.at[:, FS : 2 * FS], o_gu.at[0], out_sem.at[1]),
        pltpu.make_async_copy(gdv, o_gd.at[0], out_sem.at[2]),
    ]
    for copy in outs:
        copy.start()
    plane = jnp.concatenate(
        [part_of(z, p) + rs_take(0, 3, p) + rs_take(1, 3, p) for p in range(2)], axis=0
    ).astype(BF16)

    ysend[...] = dot(spread(NG * 16, B, 1), plane).astype(BF16).reshape(NG, 16, HD // 2)
    for i in range(1, NG):
        to = lax.rem(g + i, NG)
        send(ysend.at[to], yrecv.at[g], y2_send.at[i], y2_recv.at[g], (e, z * NG + to))
    yrecv[g] = ysend[g]
    for i in range(1, NG):
        src = lax.rem(g + i, NG)
        arrived(yrecv.at[src], y2_recv.at[src])
    halves = [sum(yrecv[y * 2 + c].astype(F32) for y in range(NY)) for c in range(2)]
    rows = jnp.concatenate([halves[0][:8], halves[0][8:], halves[1][:8], halves[1][8:]], axis=1)
    total = placing_t[:, 0:1] * rows[0:1]
    for c in range(1, CAP):
        total += placing_t[:, c : c + 1] * rows[c : c + 1]

    for s in range(NE):
        esend[s] = total[2 * s : 2 * s + 2].astype(BF16)
    for i in range(1, NE):
        to = lax.rem(e + i, NE)
        send(esend.at[to], erecv.at[e], e_send.at[i], e_recv.at[e], (to, d))
    erecv[e] = esend[e]
    for i in range(1, NE):
        src = lax.rem(e + i, NE)
        arrived(erecv.at[src], e_recv.at[src])
    o_tok[0] = sum(erecv[s].astype(F32) for s in range(NE)).astype(BF16)
    for copy in outs:
        copy.wait()
    for copy in sent:
        copy.wait_send()


def local(tokens, out_grad, expert_ids, gate_scores, w_gate, w_up, w_down):
    hbm = pl.BlockSpec(memory_space=pl.ANY)
    vmem = pl.BlockSpec(memory_space=pltpu.VMEM)
    dma = pltpu.SemaphoreType.DMA

    def like(x):
        return jax.ShapeDtypeStruct(x.shape, x.dtype)

    return pl.pallas_call(
        kernel,
        out_shape=(like(tokens), like(w_gate), like(w_up), like(w_down)),
        in_specs=[hbm, hbm, vmem, vmem, hbm, hbm, hbm],
        out_specs=(vmem, hbm, hbm, hbm),
        scratch_shapes=[
            pltpu.VMEM((NE, 2, 2, D), BF16),
            pltpu.VMEM((32, D), F32),
            pltpu.VMEM((2, 16, HD), BF16),
            pltpu.VMEM((NG, 16, HD), BF16),
            pltpu.VMEM((NZ, 2, B, HD), BF16),
            pltpu.VMEM((D, 3 * FS), BF16),
            pltpu.VMEM((FS, D), BF16),
            pltpu.VMEM((HD, 2 * FS), BF16),
            pltpu.VMEM((NZ, B, 3 * FS), BF16),
            pltpu.VMEM((NZ, CUT, 2 * FS), BF16),
            pltpu.VMEM((NZ, B, HD // 2), F32),
            pltpu.VMEM((2, 4, B, HD // 2), BF16),
            pltpu.VMEM((2, 4, B, HD // 2), BF16),
            pltpu.VMEM((NG, 16, HD // 2), BF16),
            pltpu.VMEM((NG, 16, HD // 2), BF16),
            pltpu.VMEM((NE, 2, D), BF16),
            pltpu.VMEM((NE, 2, D), BF16),
            pltpu.VMEM((D, 2 * FS), BF16),
            pltpu.VMEM((FS, D), BF16),
            dma((3,)), dma((2,)), dma((2,)), dma((2,)),
            dma((NE,)), dma((NE,)), dma((NG,)), dma((NG,)),
            dma((NZ,)), dma((NZ,)), dma((2, 4, 2)), dma((2, 4, 2)),
            dma((NZ,)), dma((NZ,)), dma((2, 4, 2)), dma((2, 4, 2)),
            dma((NG,)), dma((NG,)), dma((NE,)), dma((NE,)), dma((3,)),
        ],
        compiler_params=pltpu.CompilerParams(
            collective_id=0, has_side_effects=True, vmem_limit_bytes=50 * 2**20
        ),
        cost_estimate=pl.CostEstimate(flops=4 * 10**9, bytes_accessed=4 * 10**6, transcendentals=10**5),
    )(
        tokens, out_grad, jnp.swapaxes(expert_ids[0], 0, 1), jnp.swapaxes(gate_scores[0], 0, 1),
        w_gate, w_up, w_down,
    )


def solution(mesh):
    return jax.shard_map(
        local,
        mesh=mesh,
        in_specs=(
            P("dp", "expert", None),
            P("dp", "expert", None),
            P("dp", None, None),
            P("dp", None, None),
            P("expert", None, "dp"),
            P("expert", None, "dp"),
            P("expert", "dp", None),
        ),
        out_specs=(
            P("dp", "expert", None),
            P("expert", None, "dp"),
            P("expert", None, "dp"),
            P("expert", "dp", None),
        ),
        check_vma=False,
    )
```

```python
import jax
import jax.numpy as jnp
from jax import lax
from jax.experimental import pallas as pl
from jax.experimental.pallas import tpu as pltpu
from jax.sharding import PartitionSpec as P

MESH = pl.DeviceIdType.MESH
F32, BF16 = jnp.float32, jnp.bfloat16

NE = 8
NZ = 8
NY = 4
NG = NY * 2
CAP = 7
D = 2048
HD = D // 2
FS = 128
R = NG * CAP
B = 2 * R
Q = HD // 2
CUT = 64
NA = 1
V = Q // NA
NQ = 4
W = Q // NQ
NT = (((1,), (1,)), ((), ()))


def dot(a, b):
    return jnp.dot(a, b, preferred_element_type=F32)


def dot_nt(a, b):
    return lax.dot_general(a, b, NT, preferred_element_type=F32)


def iota(shape, dim):
    return lax.broadcasted_iota(jnp.int32, shape, dim)


def spread(rows, cols, r_dim):
    r = iota((rows, cols), r_dim)
    c = iota((rows, cols), 1 - r_dim)
    low = jnp.where(r < R, r, r - R)
    group = (low * 37) >> 8
    place = group * 9 + low + jnp.where(r < R, 0, 8)
    return jnp.where(place == c, 1.0, 0.0).astype(BF16)


def kernel(
    tok, cot, ids_in, scores_in, wg, wu, wd,
    o_tok, o_gg, o_gu, o_gd,
    ids, scores, gbuf, gf, pick, ybuf, blocks, wx, wy, wdv, wsib, stack, stack_h, ssib, part, sbuf, rbuf, ysend, yrecv, esend, erecv,
    load_sem, own_sem, ws_send, ws_recv, g_send, g_recv, y_send, y_recv, sib_send, sib_recv, ag_send, ag_recv,
    ss_send, ss_recv, rs_send, rs_recv, y2_send, y2_recv, e_send, e_recv,
):
    e = lax.axis_index("expert")
    d = lax.axis_index("dp")
    z = d // NG
    g = d - z * NG
    h = g % 2
    e_x = e // 2
    e_y = e - 2 * e_x
    across = e + 1 - 2 * e_y
    along = [lax.rem(e_x + i, NE // 2) * 2 + e_y for i in (1, 3, 2)]
    sib = (e, d + 1 - 2 * h)
    zp = (e, lax.rem(z + 1, NZ) * NG + g)
    zm = (e, lax.rem(z + NZ - 1, NZ) * NG + g)

    def wrap(k):
        return lax.rem(k + 2 * NZ, NZ)

    sent = []

    def send(src, dst, s_sem, r_sem, to):
        copy = pltpu.make_async_remote_copy(
            src_ref=src, dst_ref=dst, send_sem=s_sem, recv_sem=r_sem, device_id=to, device_id_type=MESH
        )
        copy.start()
        sent.append(copy)

    def arrived(dst, r_sem):
        pltpu.make_async_remote_copy(
            src_ref=dst, dst_ref=dst, send_sem=r_sem, recv_sem=r_sem, device_id=sib, device_id_type=MESH
        ).wait_recv()

    own = [
        pltpu.make_async_copy(tok.at[0], gbuf.at[e, 0], own_sem.at[0]),
        pltpu.make_async_copy(cot.at[0], gbuf.at[e, 1], own_sem.at[1]),
        pltpu.make_async_copy(ids_in, ids, own_sem.at[2]),
        pltpu.make_async_copy(scores_in, scores, own_sem.at[3]),
    ]
    for copy in own:
        copy.start()
    load_wd = pltpu.make_async_copy(wd.at[0], wdv, load_sem.at[8])
    load_wd.start()
    loads = []
    for n, w in enumerate((wg, wu)):
        for q in range(4):
            at = q % 2 * 2 * FS + n * FS
            loads.append(
                pltpu.make_async_copy(
                    w.at[0, q * Q : (q + 1) * Q, :], wx.at[q // 2, :, at : at + FS], load_sem.at[n * 4 + q]
                )
            )
    for copy in loads:
        copy.start()

    barrier = pltpu.get_barrier_semaphore()
    near_by = [(k, d) for k in (across, *along)]
    near_by += [(e, z * NG + lax.rem(g + i, NG)) for i in range(1, NG)] + [zp, zm]
    for to in near_by:
        pl.semaphore_signal(barrier, inc=1, device_id=to, device_id_type=MESH)
    for copy in own:
        copy.wait()
    pl.semaphore_wait(barrier, len(near_by))

    for a in range(2):
        for i, k in enumerate((across, *along)):
            send(gbuf.at[e, a], gbuf.at[e, a], g_send.at[a, i], g_recv.at[a, e], (k, d))
    for n, w in enumerate((wg, wu)):
        for f in range(2):
            rows = pl.ds(pl.multiple_of((1 - h) * HD + f * Q, Q), Q)
            send(w.at[0, rows, :], wsib.at[f, :, n * FS : (n + 1) * FS], ws_send.at[n, f], ws_recv.at[n, f], sib)

    hits = jnp.where(ids[...] == e, 1.0, 0.0)
    named_t = jnp.sum(hits, axis=0, keepdims=True)
    score_t = jnp.sum(hits * scores[...].astype(F32), axis=0, keepdims=True)
    row16, col16 = iota((16, 16), 0), iota((16, 16), 1)
    eye = jnp.where(row16 == col16, 1.0, 0.0)
    named = jnp.sum(eye * named_t, axis=1, keepdims=True)
    slot_t = jnp.sum(jnp.where(row16 < col16, named, 0.0), axis=0, keepdims=True)
    slot = jnp.sum(jnp.where(col16 < row16, named_t, 0.0), axis=1, keepdims=True)
    placing = jnp.where(slot_t == iota((8, 16), 0).astype(F32), named_t, 0.0)
    placing_t = jnp.where(slot == iota((16, 8), 1).astype(F32), named, 0.0)
    picking = (placing.astype(BF16), (placing * score_t).astype(BF16))
    gather = spread(B, NG * 16, 0)

    load_wd.wait()
    for q in range(4):
        wy[q // 2, :, q % 2 * FS : (q % 2 + 1) * FS] = wdv[:, q * Q : (q + 1) * Q].T

    for a in range(2):
        arrived(gbuf.at[across, a], g_recv.at[a, across])
        for i, k in enumerate(along):
            send(gbuf.at[across, a], gbuf.at[across, a], g_send.at[a, 4 + i], g_recv.at[a, across], (k, d))

    for a in range(2):
        for k in along:
            for src in (k, k + 1 - 2 * e_y):
                arrived(gbuf.at[src, a], g_recv.at[a, src])
        for s in range(NE):
            gf[a, 2 * s : 2 * s + 2, :] = gbuf[s, a].astype(F32)
        picked = dot(picking[a], gf[a].astype(BF16))
        for c in range(2):
            at = c * HD
            pick[a, c] = jnp.concatenate([picked[:, at : at + Q], picked[:, at + Q : at + HD]], axis=0).astype(BF16)
        for i in range(1, NG):
            to = lax.rem(g + i, NG)
            send(pick.at[a, to % 2], ybuf.at[a, g], y_send.at[a, i], y_recv.at[a, g], (e, z * NG + to))
        ybuf[a, g] = pick[a, h]

    def ag_piece(a, k, c, n):
        return blocks.at[a, k, c, :, pl.ds(n * V, V)]

    def ag_start(way, step, a, k, n):
        ref = ag_piece(a, k, h, n)
        send(ref, ref, ag_send.at[way, step, a, n], ag_recv.at[way, step, a, n], (zp, zm)[way])

    def ag_wait(way, step, a, k, n):
        arrived(ag_piece(a, k, h, n), ag_recv.at[way, step, a, n])

    def to_sibling(a, k, n):
        ref = ag_piece(a, k, h, n)
        send(ref, ref, sib_send.at[a, k, n], sib_recv.at[a, k, n], sib)

    def fwd(k):
        for a in range(2):
            for n in range(NA):
                arrived(ag_piece(a, k, 1 - h, n), sib_recv.at[a, k, n])
        r = dot(blocks[0, k, 0], wx[0]) + dot(blocks[0, k, 1], wx[1])
        pre = r[:R, : 2 * FS] + r[R:, 2 * FS :]
        r = dot(blocks[1, k, 0], wy[0]) + dot(blocks[1, k, 1], wy[1])
        gh = r[:R, :FS] + r[R:, FS:]
        gate, up = pre[:, :FS], pre[:, FS:]
        sig = jax.nn.sigmoid(gate)
        act = gate * sig
        none = jnp.zeros((R, FS), F32)
        gate_delta = gh * up * sig * (1.0 + gate * (1.0 - sig))
        for n, delta in enumerate((gate_delta, gh * act)):
            stack[k, :, n * FS : (n + 1) * FS] = jnp.concatenate([delta, none], axis=0).astype(BF16)
            stack[k, :, (n + 2) * FS : (n + 3) * FS] = jnp.concatenate([none, delta], axis=0).astype(BF16)
        hidden = act * up
        stack_h[k, :, :FS] = jnp.concatenate([hidden, none], axis=0).astype(BF16)
        stack_h[k, :, FS:] = jnp.concatenate([none, hidden], axis=0).astype(BF16)
        send(stack.at[k, 0:CUT, 0 : 2 * FS], ssib.at[k], ss_send.at[k], ss_recv.at[k], sib)

    def row_grad(k):
        arrived(ssib.at[k], ss_recv.at[k])
        delta, delta_sib = stack[k, 0:CUT, 0 : 2 * FS], ssib[k]
        part[k] = jnp.concatenate(
            [
                (dot_nt(delta, wx[h, :, f * 2 * FS : (f + 1) * 2 * FS]) + dot_nt(delta_sib, wsib[f]))[:R]
                for f in range(2)
            ],
            axis=0,
        )

    for a in range(2):
        for i in range(1, NG):
            src = lax.rem(g + i, NG)
            arrived(ybuf.at[a, src], y_recv.at[a, src])
        blocks[a, z, h] = dot(gather, ybuf[a].reshape(NG * 16, Q)).astype(BF16)
        for n in range(NA):
            for way in range(2):
                ag_start(way, 0, a, z, n)
        for n in range(NA):
            to_sibling(a, z, n)
    for copy in loads:
        copy.wait()
    for n in range(2):
        for f in range(2):
            arrived(wsib.at[f, :, n * FS : (n + 1) * FS], ws_recv.at[n, f])

    def near(way, s):
        return wrap(z - s if way == 0 else z + s)

    def lanes(q):
        return pl.ds(q * W, W)

    def rs_start(way, step, q, value):
        sbuf[way, step, :, q * W : (q + 1) * W] = value.astype(BF16)
        send(
            sbuf.at[way, step, :, lanes(q)], rbuf.at[way, step, :, lanes(q)],
            rs_send.at[way, step, q], rs_recv.at[way, step, q], (zp, zm)[way],
        )

    def rs_take(way, step, q):
        arrived(rbuf.at[way, step, :, lanes(q)], rs_recv.at[way, step, q])
        return rbuf[way, step, :, q * W : (q + 1) * W].astype(F32)

    def part_of(k, q):
        return part[k, :, q * W : (q + 1) * W]

    work = {
        (1, 0): [(fwd, z)],
        (1, 1): [],
        (2, 0): [(fwd, near(0, 1)), (row_grad, z)],
        (2, 1): [(fwd, near(1, 1))],
        (3, 0): [(fwd, near(0, 2)), (row_grad, near(0, 1))],
        (3, 1): [(fwd, near(1, 2)), (row_grad, near(1, 1))],
    }
    for s in range(1, 4):
        for a in range(2):
            for n in range(NA):
                for way in range(2):
                    ag_wait(way, s - 1, a, near(way, s), n)
                    if s < 3 or a == way:
                        ag_start(way, s, a, near(way, s), n)
                    to_sibling(a, near(way, s), n)
            for f, k in work[s, a]:
                f(k)
    far = wrap(z + 4)
    fwd(near(0, 3))
    row_grad(near(0, 2))
    fwd(near(1, 3))
    row_grad(near(1, 2))
    for n in range(NA):
        for way in range(2):
            ag_wait(way, 3, way, far, n)
            to_sibling(way, far, n)
    for way in range(2):
        row_grad(near(way, 3))

    def first(way, q):
        return (q < NQ // 2) == (way == 0)

    for q in range(NQ):
        for way in range(2):
            if not first(way, q):
                rs_start(way, 1, q, part_of(near(1 - way, 3), q))
    fwd(far)
    row_grad(far)
    for q in range(NQ):
        for way in range(2):
            if first(way, q):
                rs_start(way, 0, q, part_of(far, q))

    def weight_grad(c):
        if c == 0:
            r = dot(stack_t, blocks[0, :, 0].reshape(NZ * B, Q))
        elif c == 1:
            r = dot(stack_t, blocks[0, :, 1].reshape(NZ * B, Q))
        else:
            r = None
        if r is not None:
            for f in range(2):
                at = c * HD + f * Q
                both = r[f * 2 * FS : (f + 1) * 2 * FS].T.astype(BF16)
                o_gg[0, at : at + Q, :] = both[:, :FS]
                o_gu[0, at : at + Q, :] = both[:, FS:]
            return
        stack_ht = stack_h[...].reshape(NZ * B, 2 * FS).T
        for c in range(2):
            r = dot(stack_ht, blocks[1, :, c].reshape(NZ * B, Q))
            for f in range(2):
                at = c * HD + f * Q
                o_gd[0, :, at : at + Q] = r[f * FS : (f + 1) * FS].astype(BF16)

    stack_t = stack[...].reshape(NZ * B, 4 * FS).T
    for j in range(1, 4):
        weight_grad(j - 1)
        for q in range(NQ):
            for way in range(2):
                if j == 1 and not first(way, q):
                    continue
                rs_start(way, j, q, part_of(near(1 - way, 4 - j), q) + rs_take(way, j - 1, q))

    scatter = spread(NG * 16, B, 1)
    for q in range(2):
        plane = jnp.concatenate(
            [
                (part_of(z, p) + rs_take(0, 3, p) + rs_take(1, 3, p)).astype(BF16)
                for p in range(q * NQ // 2, (q + 1) * NQ // 2)
            ],
            axis=1,
        )
        ysend[q] = dot(scatter, plane).astype(BF16).reshape(NG, 16, Q // 2)
        for i in range(1, NG):
            to = lax.rem(g + i, NG)
            send(ysend.at[q, to], yrecv.at[q, g], y2_send.at[q, i], y2_recv.at[q, g], (e, z * NG + to))
        yrecv[q, g] = ysend[q, g]
    quarters = {}
    for q in range(2):
        for i in range(1, NG):
            src = lax.rem(g + i, NG)
            arrived(yrecv.at[q, src], y2_recv.at[q, src])
        for c in range(2):
            r = sum(yrecv[q, y * 2 + c].astype(F32) for y in range(NY))
            for f in range(2):
                quarters[c, f, q] = r[f * 8 : f * 8 + 8]
    rows = jnp.concatenate([quarters[c, f, q] for c in range(2) for f in range(2) for q in range(2)], axis=1)
    total = placing_t[:, 0:1] * rows[0:1]
    for c in range(1, CAP):
        total += placing_t[:, c : c + 1] * rows[c : c + 1]

    for s in range(NE):
        esend[s] = total[2 * s : 2 * s + 2].astype(BF16)
    for i in range(1, NE):
        to = lax.rem(e + i, NE)
        send(esend.at[to], erecv.at[e], e_send.at[i], e_recv.at[e], (to, d))
    erecv[e] = esend[e]
    for i in range(1, NE):
        src = lax.rem(e + i, NE)
        arrived(erecv.at[src], e_recv.at[src])
    o_tok[0] = sum(erecv[s].astype(F32) for s in range(NE)).astype(BF16)
    for copy in sent:
        copy.wait_send()


def write(a0, a1, a2, a3, o0, o1, o2, o3, sems):
    copies = [
        pltpu.make_async_copy(src, dst, sems.at[i])
        for i, (src, dst) in enumerate(((a0, o0), (a1, o1), (a2, o2), (a3, o3)))
    ]
    for copy in copies:
        copy.start()
    for copy in copies:
        copy.wait()


def local(tokens, out_grad, expert_ids, gate_scores, w_gate, w_up, w_down):
    hbm = pl.BlockSpec(memory_space=pl.ANY)
    far = pl.BlockSpec(memory_space=pltpu.HBM)
    vmem = pl.BlockSpec(memory_space=pltpu.VMEM)
    dma = pltpu.SemaphoreType.DMA

    def keep(x):
        return pltpu.with_memory_space_constraint(x, pltpu.HBM)

    def like(x):
        return jax.ShapeDtypeStruct(x.shape, x.dtype)

    shapes = (like(tokens), like(w_gate), like(w_up), like(w_down))
    made = pl.pallas_call(
        kernel,
        out_shape=shapes,
        in_specs=[far] * 7,
        out_specs=(vmem,) * 4,
        scratch_shapes=[
            pltpu.VMEM((2, 16), jnp.int32),
            pltpu.VMEM((2, 16), BF16),
            pltpu.VMEM((NE, 2, 2, D), BF16),
            pltpu.VMEM((2, 16, D), F32),
            pltpu.VMEM((2, 2, 16, Q), BF16),
            pltpu.VMEM((2, NG, 16, Q), BF16),
            pltpu.VMEM((2, NZ, 2, B, Q), BF16),
            pltpu.VMEM((2, Q, 4 * FS), BF16),
            pltpu.VMEM((2, Q, 2 * FS), BF16),
            pltpu.VMEM((FS, D), BF16),
            pltpu.VMEM((2, Q, 2 * FS), BF16),
            pltpu.VMEM((NZ, B, 4 * FS), BF16),
            pltpu.VMEM((NZ, B, 2 * FS), BF16),
            pltpu.VMEM((NZ, CUT, 2 * FS), BF16),
            pltpu.VMEM((NZ, B, Q), F32),
            pltpu.VMEM((2, 4, B, Q), BF16),
            pltpu.VMEM((2, 4, B, Q), BF16),
            pltpu.VMEM((2, NG, 16, Q // 2), BF16),
            pltpu.VMEM((2, NG, 16, Q // 2), BF16),
            pltpu.VMEM((NE, 2, D), BF16),
            pltpu.VMEM((NE, 2, D), BF16),
            dma((9,)), dma((4,)), dma((2, 2)), dma((2, 2)),
            dma((2, 7)), dma((2, NE)), dma((2, NG)), dma((2, NG)),
            dma((2, NZ, NA)), dma((2, NZ, NA)), dma((2, 4, 2, NA)), dma((2, 4, 2, NA)),
            dma((NZ,)), dma((NZ,)), dma((2, 4, NQ)), dma((2, 4, NQ)),
            dma((2, NG)), dma((2, NG)), dma((NE,)), dma((NE,)),
        ],
        compiler_params=pltpu.CompilerParams(
            collective_id=0, has_side_effects=True, vmem_limit_bytes=40 * 2**20
        ),
        cost_estimate=pl.CostEstimate(flops=4 * 10**9, bytes_accessed=4 * 10**6, transcendentals=10**5),
    )(
        keep(tokens), keep(out_grad), keep(jnp.swapaxes(expert_ids[0], 0, 1)), keep(jnp.swapaxes(gate_scores[0], 0, 1)),
        keep(w_gate), keep(w_up), keep(w_down),
    )
    return pl.pallas_call(
        write,
        out_shape=shapes,
        in_specs=[vmem] * 4,
        out_specs=(far,) * 4,
        scratch_shapes=[dma((4,))],
        compiler_params=pltpu.CompilerParams(vmem_limit_bytes=16 * 2**20),
    )(*made)


def solution(mesh):
    return jax.shard_map(
        local,
        mesh=mesh,
        in_specs=(
            P("dp", "expert", None),
            P("dp", "expert", None),
            P("dp", None, None),
            P("dp", None, None),
            P("expert", None, "dp"),
            P("expert", None, "dp"),
            P("expert", "dp", None),
        ),
        out_specs=(
            P("dp", "expert", None),
            P("expert", None, "dp"),
            P("expert", None, "dp"),
            P("expert", "dp", None),
        ),
        check_vma=False,
    )
```

```python
import jax
import jax.numpy as jnp
from jax import lax
from jax.experimental import pallas as pl
from jax.experimental.pallas import tpu as pltpu
from jax.sharding import PartitionSpec as P

MESH = pl.DeviceIdType.MESH
F32, BF16 = jnp.float32, jnp.bfloat16

NE = 8
NZ = 8
NY = 4
NG = NY * 2
CAP = 7
D = 2048
HD = D // 2
FS = 128
R = NG * CAP
B = 2 * R
Q = HD // 2
CUT = 64
NA = 2
V = Q // NA
NQ = 4
W = Q // NQ
NT = (((1,), (1,)), ((), ()))


def dot(a, b):
    return jnp.dot(a, b, preferred_element_type=F32)


def dot_nt(a, b):
    return lax.dot_general(a, b, NT, preferred_element_type=F32)


def iota(shape, dim):
    return lax.broadcasted_iota(jnp.int32, shape, dim)


def spread(rows, cols, r_dim):
    r = iota((rows, cols), r_dim)
    c = iota((rows, cols), 1 - r_dim)
    low = jnp.where(r < R, r, r - R)
    group = (low * 37) >> 8
    place = group * 9 + low + jnp.where(r < R, 0, 8)
    return jnp.where(place == c, 1.0, 0.0).astype(BF16)


def kernel(
    tok, cot, ids_in, scores_in, wg, wu, wd,
    o_tok, o_gg, o_gu, o_gd,
    ids, scores, gbuf, gf, pick, ybuf, blocks, wx, wy, wdv, wsib, stack, stack_h, ssib, part, sbuf, rbuf, ysend, yrecv, esend, erecv,
    load_sem, own_sem, ws_send, ws_recv, g_send, g_recv, y_send, y_recv, sib_send, sib_recv, ag_send, ag_recv,
    ss_send, ss_recv, rs_send, rs_recv, y2_send, y2_recv, e_send, e_recv,
):
    e = lax.axis_index("expert")
    d = lax.axis_index("dp")
    z = d // NG
    g = d - z * NG
    h = g % 2
    e_x = e // 2
    e_y = e - 2 * e_x
    across = e + 1 - 2 * e_y
    along = [lax.rem(e_x + i, NE // 2) * 2 + e_y for i in (1, 3, 2)]
    sib = (e, d + 1 - 2 * h)
    zp = (e, lax.rem(z + 1, NZ) * NG + g)
    zm = (e, lax.rem(z + NZ - 1, NZ) * NG + g)

    def wrap(k):
        return lax.rem(k + 2 * NZ, NZ)

    sent = []

    def send(src, dst, s_sem, r_sem, to):
        copy = pltpu.make_async_remote_copy(
            src_ref=src, dst_ref=dst, send_sem=s_sem, recv_sem=r_sem, device_id=to, device_id_type=MESH
        )
        copy.start()
        sent.append(copy)

    def arrived(dst, r_sem):
        pltpu.make_async_remote_copy(
            src_ref=dst, dst_ref=dst, send_sem=r_sem, recv_sem=r_sem, device_id=sib, device_id_type=MESH
        ).wait_recv()

    own = [
        pltpu.make_async_copy(tok.at[0], gbuf.at[e, 0], own_sem.at[0]),
        pltpu.make_async_copy(cot.at[0], gbuf.at[e, 1], own_sem.at[1]),
        pltpu.make_async_copy(ids_in, ids, own_sem.at[2]),
        pltpu.make_async_copy(scores_in, scores, own_sem.at[3]),
    ]
    for copy in own:
        copy.start()
    load_wd = pltpu.make_async_copy(wd.at[0], wdv, load_sem.at[8])
    load_wd.start()
    loads = []
    for n, w in enumerate((wg, wu)):
        for q in range(4):
            at = q % 2 * 2 * FS + n * FS
            loads.append(
                pltpu.make_async_copy(
                    w.at[0, q * Q : (q + 1) * Q, :], wx.at[q // 2, :, at : at + FS], load_sem.at[n * 4 + q]
                )
            )
    for copy in loads:
        copy.start()

    barrier = pltpu.get_barrier_semaphore()
    near_by = [(k, d) for k in (across, *along)]
    near_by += [(e, z * NG + lax.rem(g + i, NG)) for i in range(1, NG)] + [zp, zm]
    for to in near_by:
        pl.semaphore_signal(barrier, inc=1, device_id=to, device_id_type=MESH)
    for copy in own:
        copy.wait()
    pl.semaphore_wait(barrier, len(near_by))

    for a in range(2):
        for i, k in enumerate((across, *along)):
            send(gbuf.at[e, a], gbuf.at[e, a], g_send.at[a, i], g_recv.at[a, e], (k, d))
    for n, w in enumerate((wg, wu)):
        for f in range(2):
            rows = pl.ds(pl.multiple_of((1 - h) * HD + f * Q, Q), Q)
            send(w.at[0, rows, :], wsib.at[f, :, n * FS : (n + 1) * FS], ws_send.at[n, f], ws_recv.at[n, f], sib)

    hits = jnp.where(ids[...] == e, 1.0, 0.0)
    named_t = jnp.sum(hits, axis=0, keepdims=True)
    score_t = jnp.sum(hits * scores[...].astype(F32), axis=0, keepdims=True)
    row16, col16 = iota((16, 16), 0), iota((16, 16), 1)
    eye = jnp.where(row16 == col16, 1.0, 0.0)
    named = jnp.sum(eye * named_t, axis=1, keepdims=True)
    slot_t = jnp.sum(jnp.where(row16 < col16, named, 0.0), axis=0, keepdims=True)
    slot = jnp.sum(jnp.where(col16 < row16, named_t, 0.0), axis=1, keepdims=True)
    placing = jnp.where(slot_t == iota((8, 16), 0).astype(F32), named_t, 0.0)
    placing_t = jnp.where(slot == iota((16, 8), 1).astype(F32), named, 0.0)
    picking = (placing.astype(BF16), (placing * score_t).astype(BF16))
    gather = spread(B, NG * 16, 0)

    load_wd.wait()
    for q in range(4):
        wy[q // 2, :, q % 2 * FS : (q % 2 + 1) * FS] = wdv[:, q * Q : (q + 1) * Q].T

    for a in range(2):
        arrived(gbuf.at[across, a], g_recv.at[a, across])
        for i, k in enumerate(along):
            send(gbuf.at[across, a], gbuf.at[across, a], g_send.at[a, 4 + i], g_recv.at[a, across], (k, d))

    for a in range(2):
        for k in along:
            for src in (k, k + 1 - 2 * e_y):
                arrived(gbuf.at[src, a], g_recv.at[a, src])
        for s in range(NE):
            gf[a, 2 * s : 2 * s + 2, :] = gbuf[s, a].astype(F32)
        picked = dot(picking[a], gf[a].astype(BF16))
        for c in range(2):
            at = c * HD
            both = jnp.concatenate([picked[:, at : at + Q], picked[:, at + Q : at + HD]], axis=0).astype(BF16)
            for n in range(NA):
                pick[a, n, c] = both[:, n * V : (n + 1) * V]
        for n in range(NA):
            for i in range(1, NG):
                to = lax.rem(g + i, NG)
                send(
                    pick.at[a, n, to % 2], ybuf.at[a, n, g], y_send.at[a, n, i], y_recv.at[a, n, g],
                    (e, z * NG + to),
                )
            ybuf[a, n, g] = pick[a, n, h]

    def ag_piece(a, k, c, n):
        return blocks.at[a, k, c, :, pl.ds(n * V, V)]

    def ag_start(way, step, a, k, n):
        ref = ag_piece(a, k, h, n)
        send(ref, ref, ag_send.at[way, step, a, n], ag_recv.at[way, step, a, n], (zp, zm)[way])

    def ag_wait(way, step, a, k, n):
        arrived(ag_piece(a, k, h, n), ag_recv.at[way, step, a, n])

    def to_sibling(a, k, n):
        ref = ag_piece(a, k, h, n)
        send(ref, ref, sib_send.at[a, k, n], sib_recv.at[a, k, n], sib)

    def fwd(k):
        for a in range(2):
            for n in range(NA):
                arrived(ag_piece(a, k, 1 - h, n), sib_recv.at[a, k, n])
        r = dot(blocks[0, k, 0], wx[0]) + dot(blocks[0, k, 1], wx[1])
        pre = r[:R, : 2 * FS] + r[R:, 2 * FS :]
        r = dot(blocks[1, k, 0], wy[0]) + dot(blocks[1, k, 1], wy[1])
        gh = r[:R, :FS] + r[R:, FS:]
        gate, up = pre[:, :FS], pre[:, FS:]
        sig = jax.nn.sigmoid(gate)
        act = gate * sig
        none = jnp.zeros((R, FS), F32)
        gate_delta = gh * up * sig * (1.0 + gate * (1.0 - sig))
        for n, delta in enumerate((gate_delta, gh * act)):
            stack[k, :, n * FS : (n + 1) * FS] = jnp.concatenate([delta, none], axis=0).astype(BF16)
            stack[k, :, (n + 2) * FS : (n + 3) * FS] = jnp.concatenate([none, delta], axis=0).astype(BF16)
        hidden = act * up
        stack_h[k, :, :FS] = jnp.concatenate([hidden, none], axis=0).astype(BF16)
        stack_h[k, :, FS:] = jnp.concatenate([none, hidden], axis=0).astype(BF16)
        send(stack.at[k, 0:CUT, 0 : 2 * FS], ssib.at[k], ss_send.at[k], ss_recv.at[k], sib)

    def row_grad(k):
        arrived(ssib.at[k], ss_recv.at[k])
        delta, delta_sib = stack[k, 0:CUT, 0 : 2 * FS], ssib[k]
        part[k] = jnp.concatenate(
            [
                (dot_nt(delta, wx[h, :, f * 2 * FS : (f + 1) * 2 * FS]) + dot_nt(delta_sib, wsib[f]))[:R]
                for f in range(2)
            ],
            axis=0,
        )

    for a in range(2):
        for n in range(NA):
            for i in range(1, NG):
                src = lax.rem(g + i, NG)
                arrived(ybuf.at[a, n, src], y_recv.at[a, n, src])
            blocks[a, z, h, :, n * V : (n + 1) * V] = dot(gather, ybuf[a, n].reshape(NG * 16, V)).astype(BF16)
            for way in range(2):
                ag_start(way, 0, a, z, n)
            to_sibling(a, z, n)
    for copy in loads:
        copy.wait()
    for n in range(2):
        for f in range(2):
            arrived(wsib.at[f, :, n * FS : (n + 1) * FS], ws_recv.at[n, f])

    def near(way, s):
        return wrap(z - s if way == 0 else z + s)

    def lanes(q):
        return pl.ds(q * W, W)

    def rs_start(way, step, q, value):
        sbuf[way, step, :, q * W : (q + 1) * W] = value.astype(BF16)
        send(
            sbuf.at[way, step, :, lanes(q)], rbuf.at[way, step, :, lanes(q)],
            rs_send.at[way, step, q], rs_recv.at[way, step, q], (zp, zm)[way],
        )

    def rs_take(way, step, q):
        arrived(rbuf.at[way, step, :, lanes(q)], rs_recv.at[way, step, q])
        return rbuf[way, step, :, q * W : (q + 1) * W].astype(F32)

    def part_of(k, q):
        return part[k, :, q * W : (q + 1) * W]

    work = {
        (1, 0): [(fwd, z)],
        (1, 1): [],
        (2, 0): [(fwd, near(0, 1)), (row_grad, z)],
        (2, 1): [(fwd, near(1, 1))],
        (3, 0): [(fwd, near(0, 2)), (row_grad, near(0, 1))],
        (3, 1): [(fwd, near(1, 2)), (row_grad, near(1, 1))],
    }
    for s in range(1, 4):
        for a in range(2):
            for n in range(NA):
                for way in range(2):
                    ag_wait(way, s - 1, a, near(way, s), n)
                    if s < 3 or a == way:
                        ag_start(way, s, a, near(way, s), n)
                    to_sibling(a, near(way, s), n)
            for f, k in work[s, a]:
                f(k)
    far = wrap(z + 4)
    fwd(near(0, 3))
    row_grad(near(0, 2))
    fwd(near(1, 3))
    row_grad(near(1, 2))
    for n in range(NA):
        for way in range(2):
            ag_wait(way, 3, way, far, n)
            to_sibling(way, far, n)
    for way in range(2):
        row_grad(near(way, 3))

    def first(way, q):
        return q % 2 == way

    for q in range(NQ):
        for way in range(2):
            if not first(way, q):
                rs_start(way, 1, q, part_of(near(1 - way, 3), q))
    fwd(far)
    row_grad(far)
    for q in range(NQ):
        for way in range(2):
            if first(way, q):
                rs_start(way, 0, q, part_of(far, q))

    def weight_grad(c):
        if c == 0:
            r = dot(stack_t, blocks[0, :, 0].reshape(NZ * B, Q))
        elif c == 1:
            r = dot(stack_t, blocks[0, :, 1].reshape(NZ * B, Q))
        else:
            r = None
        if r is not None:
            for f in range(2):
                at = c * HD + f * Q
                both = r[f * 2 * FS : (f + 1) * 2 * FS].T.astype(BF16)
                o_gg[0, at : at + Q, :] = both[:, :FS]
                o_gu[0, at : at + Q, :] = both[:, FS:]
            return
        stack_ht = stack_h[...].reshape(NZ * B, 2 * FS).T
        for c in range(2):
            r = dot(stack_ht, blocks[1, :, c].reshape(NZ * B, Q))
            for f in range(2):
                at = c * HD + f * Q
                o_gd[0, :, at : at + Q] = r[f * FS : (f + 1) * FS].astype(BF16)

    stack_t = stack[...].reshape(NZ * B, 4 * FS).T
    for j in range(1, 4):
        weight_grad(j - 1)
        for q in range(NQ):
            for way in range(2):
                if j == 1 and not first(way, q):
                    continue
                rs_start(way, j, q, part_of(near(1 - way, 4 - j), q) + rs_take(way, j - 1, q))

    scatter = spread(NG * 16, B, 1)
    for q in range(2):
        plane = jnp.concatenate(
            [
                (part_of(z, p) + rs_take(0, 3, p) + rs_take(1, 3, p)).astype(BF16)
                for p in range(q * NQ // 2, (q + 1) * NQ // 2)
            ],
            axis=1,
        )
        ysend[q] = dot(scatter, plane).astype(BF16).reshape(NG, 16, Q // 2)
        for i in range(1, NG):
            to = lax.rem(g + i, NG)
            send(ysend.at[q, to], yrecv.at[q, g], y2_send.at[q, i], y2_recv.at[q, g], (e, z * NG + to))
        yrecv[q, g] = ysend[q, g]
    early = len(sent)
    for q in range(2):
        for i in range(1, NG):
            src = lax.rem(g + i, NG)
            arrived(yrecv.at[q, src], y2_recv.at[q, src])
        rows = []
        for c in range(2):
            r = sum(yrecv[q, y * 2 + c].astype(F32) for y in range(NY))
            rows += [r[:8], r[8:]]
        rows = jnp.concatenate(rows, axis=1)
        total = placing_t[:, 0:1] * rows[0:1]
        for c in range(1, CAP):
            total += placing_t[:, c : c + 1] * rows[c : c + 1]
        for s in range(NE):
            esend[q, s] = total[2 * s : 2 * s + 2].astype(BF16)
        for i in range(1, NE):
            to = lax.rem(e + i, NE)
            send(esend.at[q, to], erecv.at[q, e], e_send.at[q, i], e_recv.at[q, e], (to, d))
        erecv[q, e] = esend[q, e]
    for copy in sent[:early]:
        copy.wait_send()
    for q in range(2):
        for i in range(1, NE):
            src = lax.rem(e + i, NE)
            arrived(erecv.at[q, src], e_recv.at[q, src])
        token = sum(erecv[q, s].astype(F32) for s in range(NE)).astype(BF16)
        for n in range(4):
            at = n * Q + q * (Q // 2)
            o_tok[0, :, at : at + Q // 2] = token[:, n * (Q // 2) : (n + 1) * (Q // 2)]
    for copy in sent[early:]:
        copy.wait_send()


def write(a0, a1, a2, a3, o0, o1, o2, o3, sems):
    copies = [
        pltpu.make_async_copy(src, dst, sems.at[i])
        for i, (src, dst) in enumerate(((a0, o0), (a1, o1), (a2, o2), (a3, o3)))
    ]
    for copy in copies:
        copy.start()
    for copy in copies:
        copy.wait()


def local(tokens, out_grad, expert_ids, gate_scores, w_gate, w_up, w_down):
    hbm = pl.BlockSpec(memory_space=pl.ANY)
    far = pl.BlockSpec(memory_space=pltpu.HBM)
    vmem = pl.BlockSpec(memory_space=pltpu.VMEM)
    dma = pltpu.SemaphoreType.DMA

    def keep(x):
        return pltpu.with_memory_space_constraint(x, pltpu.HBM)

    def like(x):
        return jax.ShapeDtypeStruct(x.shape, x.dtype)

    shapes = (like(tokens), like(w_gate), like(w_up), like(w_down))
    made = pl.pallas_call(
        kernel,
        out_shape=shapes,
        in_specs=[far] * 7,
        out_specs=(vmem,) * 4,
        scratch_shapes=[
            pltpu.VMEM((2, 16), jnp.int32),
            pltpu.VMEM((2, 16), BF16),
            pltpu.VMEM((NE, 2, 2, D), BF16),
            pltpu.VMEM((2, 16, D), F32),
            pltpu.VMEM((2, NA, 2, 16, V), BF16),
            pltpu.VMEM((2, NA, NG, 16, V), BF16),
            pltpu.VMEM((2, NZ, 2, B, Q), BF16),
            pltpu.VMEM((2, Q, 4 * FS), BF16),
            pltpu.VMEM((2, Q, 2 * FS), BF16),
            pltpu.VMEM((FS, D), BF16),
            pltpu.VMEM((2, Q, 2 * FS), BF16),
            pltpu.VMEM((NZ, B, 4 * FS), BF16),
            pltpu.VMEM((NZ, B, 2 * FS), BF16),
            pltpu.VMEM((NZ, CUT, 2 * FS), BF16),
            pltpu.VMEM((NZ, B, Q), F32),
            pltpu.VMEM((2, 4, B, Q), BF16),
            pltpu.VMEM((2, 4, B, Q), BF16),
            pltpu.VMEM((2, NG, 16, Q // 2), BF16),
            pltpu.VMEM((2, NG, 16, Q // 2), BF16),
            pltpu.VMEM((2, NE, 2, HD), BF16),
            pltpu.VMEM((2, NE, 2, HD), BF16),
            dma((9,)), dma((4,)), dma((2, 2)), dma((2, 2)),
            dma((2, 7)), dma((2, NE)), dma((2, NA, NG)), dma((2, NA, NG)),
            dma((2, NZ, NA)), dma((2, NZ, NA)), dma((2, 4, 2, NA)), dma((2, 4, 2, NA)),
            dma((NZ,)), dma((NZ,)), dma((2, 4, NQ)), dma((2, 4, NQ)),
            dma((2, NG)), dma((2, NG)), dma((2, NE)), dma((2, NE)),
        ],
        compiler_params=pltpu.CompilerParams(
            collective_id=0, has_side_effects=True, vmem_limit_bytes=40 * 2**20
        ),
        cost_estimate=pl.CostEstimate(flops=4 * 10**9, bytes_accessed=4 * 10**6, transcendentals=10**5),
    )(
        keep(tokens), keep(out_grad), keep(jnp.swapaxes(expert_ids[0], 0, 1)), keep(jnp.swapaxes(gate_scores[0], 0, 1)),
        keep(w_gate), keep(w_up), keep(w_down),
    )
    return pl.pallas_call(
        write,
        out_shape=shapes,
        in_specs=[vmem] * 4,
        out_specs=(far,) * 4,
        scratch_shapes=[dma((4,))],
        compiler_params=pltpu.CompilerParams(vmem_limit_bytes=16 * 2**20),
    )(*made)


def solution(mesh):
    return jax.shard_map(
        local,
        mesh=mesh,
        in_specs=(
            P("dp", "expert", None),
            P("dp", "expert", None),
            P("dp", None, None),
            P("dp", None, None),
            P("expert", None, "dp"),
            P("expert", None, "dp"),
            P("expert", "dp", None),
        ),
        out_specs=(
            P("dp", "expert", None),
            P("expert", None, "dp"),
            P("expert", None, "dp"),
            P("expert", "dp", None),
        ),
        check_vma=False,
    )
```

```python
import jax
import jax.numpy as jnp
from jax import lax
from jax.experimental import pallas as pl
from jax.experimental.pallas import tpu as pltpu
from jax.sharding import PartitionSpec as P

MESH = pl.DeviceIdType.MESH
F32, BF16 = jnp.float32, jnp.bfloat16

NE = 8
NZ = 8
NY = 4
NG = NY * 2
CAP = 7
D = 2048
HD = D // 2
FS = 128
R = NG * CAP
B = 2 * R
Q = HD // 2
CUT = 64
NA = 2
V = Q // NA
NQ = 4
W = Q // NQ
NT = (((1,), (1,)), ((), ()))


def dot(a, b):
    return jnp.dot(a, b, preferred_element_type=F32)


def dot_nt(a, b):
    return lax.dot_general(a, b, NT, preferred_element_type=F32)


def iota(shape, dim):
    return lax.broadcasted_iota(jnp.int32, shape, dim)


def spread(rows, cols, r_dim):
    r = iota((rows, cols), r_dim)
    c = iota((rows, cols), 1 - r_dim)
    low = jnp.where(r < R, r, r - R)
    group = (low * 37) >> 8
    place = group * 9 + low + jnp.where(r < R, 0, 8)
    return jnp.where(place == c, 1.0, 0.0).astype(BF16)


def kernel(
    tok, cot, ids_in, scores_in, wg, wu, wd,
    o_tok, o_gg, o_gu, o_gd,
    ids, scores, gbuf, gf, pick, ybuf, blocks, wx, wy, wdv, wsib, stack, stack_h, ssib, part, sbuf, rbuf, ysend, yrecv, esend, erecv,
    load_sem, own_sem, ws_send, ws_recv, g_send, g_recv, y_send, y_recv, sib_send, sib_recv, ag_send, ag_recv,
    ss_send, ss_recv, rs_send, rs_recv, y2_send, y2_recv, e_send, e_recv,
):
    e = lax.axis_index("expert")
    d = lax.axis_index("dp")
    z = d // NG
    g = d - z * NG
    h = g % 2
    e_x = e // 2
    e_y = e - 2 * e_x
    across = e + 1 - 2 * e_y
    along = [lax.rem(e_x + i, NE // 2) * 2 + e_y for i in (1, 3, 2)]
    sib = (e, d + 1 - 2 * h)
    zp = (e, lax.rem(z + 1, NZ) * NG + g)
    zm = (e, lax.rem(z + NZ - 1, NZ) * NG + g)

    def wrap(k):
        return lax.rem(k + 2 * NZ, NZ)

    sent = []

    def send(src, dst, s_sem, r_sem, to):
        copy = pltpu.make_async_remote_copy(
            src_ref=src, dst_ref=dst, send_sem=s_sem, recv_sem=r_sem, device_id=to, device_id_type=MESH
        )
        copy.start()
        sent.append(copy)

    def arrived(dst, r_sem):
        pltpu.make_async_remote_copy(
            src_ref=dst, dst_ref=dst, send_sem=r_sem, recv_sem=r_sem, device_id=sib, device_id_type=MESH
        ).wait_recv()

    barrier = pltpu.get_barrier_semaphore()
    near_by = [(k, d) for k in (across, *along)]
    near_by += [(e, z * NG + lax.rem(g + i, NG)) for i in range(1, NG)] + [zp, zm]
    for to in near_by:
        pl.semaphore_signal(barrier, inc=1, device_id=to, device_id_type=MESH)

    own = [
        pltpu.make_async_copy(tok.at[0], gbuf.at[e, 0], own_sem.at[0]),
        pltpu.make_async_copy(cot.at[0], gbuf.at[e, 1], own_sem.at[1]),
        pltpu.make_async_copy(ids_in, ids, own_sem.at[2]),
        pltpu.make_async_copy(scores_in, scores, own_sem.at[3]),
    ]
    for copy in own:
        copy.start()
    load_wd = pltpu.make_async_copy(wd.at[0], wdv, load_sem.at[8])
    load_wd.start()
    loads = []
    for n, w in enumerate((wg, wu)):
        for q in range(4):
            at = q % 2 * 2 * FS + n * FS
            loads.append(
                pltpu.make_async_copy(
                    w.at[0, q * Q : (q + 1) * Q, :], wx.at[q // 2, :, at : at + FS], load_sem.at[n * 4 + q]
                )
            )
    for copy in loads:
        copy.start()

    for copy in own:
        copy.wait()
    pl.semaphore_wait(barrier, len(near_by))

    for a in range(2):
        for i, k in enumerate((across, *along)):
            send(gbuf.at[e, a], gbuf.at[e, a], g_send.at[a, i], g_recv.at[a, e], (k, d))
    for n, w in enumerate((wg, wu)):
        for f in range(2):
            rows = pl.ds(pl.multiple_of((1 - h) * HD + f * Q, Q), Q)
            send(w.at[0, rows, :], wsib.at[f, :, n * FS : (n + 1) * FS], ws_send.at[n, f], ws_recv.at[n, f], sib)

    hits = jnp.where(ids[...] == e, 1.0, 0.0)
    named_t = jnp.sum(hits, axis=0, keepdims=True)
    score_t = jnp.sum(hits * scores[...].astype(F32), axis=0, keepdims=True)
    row16, col16 = iota((16, 16), 0), iota((16, 16), 1)
    eye = jnp.where(row16 == col16, 1.0, 0.0)
    named = jnp.sum(eye * named_t, axis=1, keepdims=True)
    slot_t = jnp.sum(jnp.where(row16 < col16, named, 0.0), axis=0, keepdims=True)
    slot = jnp.sum(jnp.where(col16 < row16, named_t, 0.0), axis=1, keepdims=True)
    placing = jnp.where(slot_t == iota((8, 16), 0).astype(F32), named_t, 0.0)
    placing_t = jnp.where(slot == iota((16, 8), 1).astype(F32), named, 0.0)
    picking = (placing.astype(BF16), (placing * score_t).astype(BF16))
    gather = spread(B, NG * 16, 0)

    load_wd.wait()
    for q in range(4):
        wy[q // 2, :, q % 2 * FS : (q % 2 + 1) * FS] = wdv[:, q * Q : (q + 1) * Q].T

    for a in range(2):
        arrived(gbuf.at[across, a], g_recv.at[a, across])
        for i, k in enumerate(along):
            send(gbuf.at[across, a], gbuf.at[across, a], g_send.at[a, 4 + i], g_recv.at[a, across], (k, d))

    for a in range(2):
        for k in along:
            for src in (k, k + 1 - 2 * e_y):
                arrived(gbuf.at[src, a], g_recv.at[a, src])
        for s in range(NE):
            gf[a, 2 * s : 2 * s + 2, :] = gbuf[s, a].astype(F32)
        picked = dot(picking[a], gf[a].astype(BF16))
        for c in range(2):
            at = c * HD
            both = jnp.concatenate([picked[:, at : at + Q], picked[:, at + Q : at + HD]], axis=0).astype(BF16)
            for n in range(NA):
                pick[a, n, c] = both[:, n * V : (n + 1) * V]
        for n in range(NA):
            for i in range(1, NG):
                to = lax.rem(g + i, NG)
                send(
                    pick.at[a, n, to % 2], ybuf.at[a, n, g], y_send.at[a, n, i], y_recv.at[a, n, g],
                    (e, z * NG + to),
                )
            ybuf[a, n, g] = pick[a, n, h]

    def ag_piece(a, k, c, n):
        return blocks.at[a, k, c, :, pl.ds(n * V, V)]

    def ag_start(way, step, a, k, n):
        ref = ag_piece(a, k, h, n)
        send(ref, ref, ag_send.at[way, step, a, n], ag_recv.at[way, step, a, n], (zp, zm)[way])

    def ag_wait(way, step, a, k, n):
        arrived(ag_piece(a, k, h, n), ag_recv.at[way, step, a, n])

    def to_sibling(a, k, n):
        ref = ag_piece(a, k, h, n)
        send(ref, ref, sib_send.at[a, k, n], sib_recv.at[a, k, n], sib)

    def fwd(k):
        for a in range(2):
            for n in range(NA):
                arrived(ag_piece(a, k, 1 - h, n), sib_recv.at[a, k, n])
        r = dot(blocks[0, k, 0], wx[0]) + dot(blocks[0, k, 1], wx[1])
        pre = r[:R, : 2 * FS] + r[R:, 2 * FS :]
        r = dot(blocks[1, k, 0], wy[0]) + dot(blocks[1, k, 1], wy[1])
        gh = r[:R, :FS] + r[R:, FS:]
        gate, up = pre[:, :FS], pre[:, FS:]
        sig = jax.nn.sigmoid(gate)
        act = gate * sig
        none = jnp.zeros((R, FS), F32)
        gate_delta = gh * up * sig * (1.0 + gate * (1.0 - sig))
        for n, delta in enumerate((gate_delta, gh * act)):
            stack[k, :, n * FS : (n + 1) * FS] = jnp.concatenate([delta, none], axis=0).astype(BF16)
            stack[k, :, (n + 2) * FS : (n + 3) * FS] = jnp.concatenate([none, delta], axis=0).astype(BF16)
        hidden = act * up
        stack_h[k, :, :FS] = jnp.concatenate([hidden, none], axis=0).astype(BF16)
        stack_h[k, :, FS:] = jnp.concatenate([none, hidden], axis=0).astype(BF16)
        send(stack.at[k, 0:CUT, 0 : 2 * FS], ssib.at[k], ss_send.at[k], ss_recv.at[k], sib)

    def row_grad(k):
        arrived(ssib.at[k], ss_recv.at[k])
        delta, delta_sib = stack[k, 0:CUT, 0 : 2 * FS], ssib[k]
        part[k] = jnp.concatenate(
            [
                (dot_nt(delta, wx[h, :, f * 2 * FS : (f + 1) * 2 * FS]) + dot_nt(delta_sib, wsib[f]))[:R]
                for f in range(2)
            ],
            axis=0,
        )

    for a in range(2):
        for n in range(NA):
            for i in range(1, NG):
                src = lax.rem(g + i, NG)
                arrived(ybuf.at[a, n, src], y_recv.at[a, n, src])
            blocks[a, z, h, :, n * V : (n + 1) * V] = dot(gather, ybuf[a, n].reshape(NG * 16, V)).astype(BF16)
            for way in range(2):
                ag_start(way, 0, a, z, n)
            to_sibling(a, z, n)
    for copy in loads:
        copy.wait()
    for n in range(2):
        for f in range(2):
            arrived(wsib.at[f, :, n * FS : (n + 1) * FS], ws_recv.at[n, f])

    def near(way, s):
        return wrap(z - s if way == 0 else z + s)

    def lanes(q):
        return pl.ds(q * W, W)

    def rs_start(way, step, q, value):
        sbuf[way, step, :, q * W : (q + 1) * W] = value.astype(BF16)
        send(
            sbuf.at[way, step, :, lanes(q)], rbuf.at[way, step, :, lanes(q)],
            rs_send.at[way, step, q], rs_recv.at[way, step, q], (zp, zm)[way],
        )

    def rs_take(way, step, q):
        arrived(rbuf.at[way, step, :, lanes(q)], rs_recv.at[way, step, q])
        return rbuf[way, step, :, q * W : (q + 1) * W].astype(F32)

    def part_of(k, q):
        return part[k, :, q * W : (q + 1) * W]

    work = {
        (1, 0): [(fwd, z)],
        (1, 1): [],
        (2, 0): [(fwd, near(0, 1)), (row_grad, z)],
        (2, 1): [(fwd, near(1, 1))],
        (3, 0): [(fwd, near(0, 2)), (row_grad, near(0, 1))],
        (3, 1): [(fwd, near(1, 2)), (row_grad, near(1, 1))],
    }
    for s in range(1, 4):
        for a in range(2):
            for n in range(NA):
                for way in range(2):
                    ag_wait(way, s - 1, a, near(way, s), n)
                    if s < 3 or a == way:
                        ag_start(way, s, a, near(way, s), n)
                    to_sibling(a, near(way, s), n)
            for f, k in work[s, a]:
                f(k)
    far = wrap(z + 4)
    fwd(near(0, 3))
    fwd(near(1, 3))
    for n in range(NA):
        for way in range(2):
            ag_wait(way, 3, way, far, n)
            to_sibling(way, far, n)
    for way in range(2):
        row_grad(near(way, 3))

    def first(way, q):
        return q % 2 == way

    for q in range(NQ):
        for way in range(2):
            if not first(way, q):
                rs_start(way, 1, q, part_of(near(1 - way, 3), q))
    fwd(far)
    row_grad(near(0, 2))
    row_grad(near(1, 2))
    row_grad(far)
    for q in range(NQ):
        for way in range(2):
            if first(way, q):
                rs_start(way, 0, q, part_of(far, q))

    def weight_grad(c):
        if c == 0:
            r = dot(stack_t, blocks[0, :, 0].reshape(NZ * B, Q))
        elif c == 1:
            r = dot(stack_t, blocks[0, :, 1].reshape(NZ * B, Q))
        else:
            r = None
        if r is not None:
            for f in range(2):
                at = c * HD + f * Q
                both = r[f * 2 * FS : (f + 1) * 2 * FS].T.astype(BF16)
                o_gg[0, at : at + Q, :] = both[:, :FS]
                o_gu[0, at : at + Q, :] = both[:, FS:]
            return
        stack_ht = stack_h[...].reshape(NZ * B, 2 * FS).T
        for c in range(2):
            r = dot(stack_ht, blocks[1, :, c].reshape(NZ * B, Q))
            for f in range(2):
                at = c * HD + f * Q
                o_gd[0, :, at : at + Q] = r[f * FS : (f + 1) * FS].astype(BF16)

    stack_t = stack[...].reshape(NZ * B, 4 * FS).T
    for j in range(1, 4):
        weight_grad(j - 1)
        for q in range(NQ):
            for way in range(2):
                if j == 1 and not first(way, q):
                    continue
                rs_start(way, j, q, part_of(near(1 - way, 4 - j), q) + rs_take(way, j - 1, q))

    scatter = spread(NG * 16, B, 1)
    for q in range(2):
        plane = jnp.concatenate(
            [
                (part_of(z, p) + rs_take(0, 3, p) + rs_take(1, 3, p)).astype(BF16)
                for p in range(q * NQ // 2, (q + 1) * NQ // 2)
            ],
            axis=1,
        )
        ysend[q] = dot(scatter, plane).astype(BF16).reshape(NG, 16, Q // 2)
        for i in range(1, NG):
            to = lax.rem(g + i, NG)
            send(ysend.at[q, to], yrecv.at[q, g], y2_send.at[q, i], y2_recv.at[q, g], (e, z * NG + to))
        yrecv[q, g] = ysend[q, g]
    early = len(sent)
    for q in range(2):
        for i in range(1, NG):
            src = lax.rem(g + i, NG)
            arrived(yrecv.at[q, src], y2_recv.at[q, src])
        rows = []
        for c in range(2):
            r = sum(yrecv[q, y * 2 + c].astype(F32) for y in range(NY))
            rows += [r[:8], r[8:]]
        rows = jnp.concatenate(rows, axis=1)
        total = placing_t[:, 0:1] * rows[0:1]
        for c in range(1, CAP):
            total += placing_t[:, c : c + 1] * rows[c : c + 1]
        for s in range(NE):
            esend[q, s] = total[2 * s : 2 * s + 2].astype(BF16)
        for i in range(1, NE):
            to = lax.rem(e + i, NE)
            send(esend.at[q, to], erecv.at[q, e], e_send.at[q, i], e_recv.at[q, e], (to, d))
        erecv[q, e] = esend[q, e]
    for copy in sent[:early]:
        copy.wait_send()
    for q in range(2):
        for i in range(1, NE):
            src = lax.rem(e + i, NE)
            arrived(erecv.at[q, src], e_recv.at[q, src])
        token = sum(erecv[q, s].astype(F32) for s in range(NE)).astype(BF16)
        for n in range(4):
            at = n * Q + q * (Q // 2)
            o_tok[0, :, at : at + Q // 2] = token[:, n * (Q // 2) : (n + 1) * (Q // 2)]
    for copy in sent[early:]:
        copy.wait_send()


def write(a0, a1, a2, a3, o0, o1, o2, o3, sems):
    copies = [
        pltpu.make_async_copy(src, dst, sems.at[i])
        for i, (src, dst) in enumerate(((a0, o0), (a1, o1), (a2, o2), (a3, o3)))
    ]
    for copy in copies:
        copy.start()
    for copy in copies:
        copy.wait()


def local(tokens, out_grad, expert_ids, gate_scores, w_gate, w_up, w_down):
    hbm = pl.BlockSpec(memory_space=pl.ANY)
    far = pl.BlockSpec(memory_space=pltpu.HBM)
    vmem = pl.BlockSpec(memory_space=pltpu.VMEM)
    dma = pltpu.SemaphoreType.DMA

    def keep(x):
        return pltpu.with_memory_space_constraint(x, pltpu.HBM)

    def like(x):
        return jax.ShapeDtypeStruct(x.shape, x.dtype)

    shapes = (like(tokens), like(w_gate), like(w_up), like(w_down))
    made = pl.pallas_call(
        kernel,
        out_shape=shapes,
        in_specs=[far] * 7,
        out_specs=(vmem,) * 4,
        scratch_shapes=[
            pltpu.VMEM((2, 16), jnp.int32),
            pltpu.VMEM((2, 16), BF16),
            pltpu.VMEM((NE, 2, 2, D), BF16),
            pltpu.VMEM((2, 16, D), F32),
            pltpu.VMEM((2, NA, 2, 16, V), BF16),
            pltpu.VMEM((2, NA, NG, 16, V), BF16),
            pltpu.VMEM((2, NZ, 2, B, Q), BF16),
            pltpu.VMEM((2, Q, 4 * FS), BF16),
            pltpu.VMEM((2, Q, 2 * FS), BF16),
            pltpu.VMEM((FS, D), BF16),
            pltpu.VMEM((2, Q, 2 * FS), BF16),
            pltpu.VMEM((NZ, B, 4 * FS), BF16),
            pltpu.VMEM((NZ, B, 2 * FS), BF16),
            pltpu.VMEM((NZ, CUT, 2 * FS), BF16),
            pltpu.VMEM((NZ, B, Q), F32),
            pltpu.VMEM((2, 4, B, Q), BF16),
            pltpu.VMEM((2, 4, B, Q), BF16),
            pltpu.VMEM((2, NG, 16, Q // 2), BF16),
            pltpu.VMEM((2, NG, 16, Q // 2), BF16),
            pltpu.VMEM((2, NE, 2, HD), BF16),
            pltpu.VMEM((2, NE, 2, HD), BF16),
            dma((9,)), dma((4,)), dma((2, 2)), dma((2, 2)),
            dma((2, 7)), dma((2, NE)), dma((2, NA, NG)), dma((2, NA, NG)),
            dma((2, NZ, NA)), dma((2, NZ, NA)), dma((2, 4, 2, NA)), dma((2, 4, 2, NA)),
            dma((NZ,)), dma((NZ,)), dma((2, 4, NQ)), dma((2, 4, NQ)),
            dma((2, NG)), dma((2, NG)), dma((2, NE)), dma((2, NE)),
        ],
        compiler_params=pltpu.CompilerParams(
            collective_id=0, has_side_effects=True, vmem_limit_bytes=40 * 2**20
        ),
        cost_estimate=pl.CostEstimate(flops=4 * 10**9, bytes_accessed=4 * 10**6, transcendentals=10**5),
    )(
        keep(tokens), keep(out_grad), keep(jnp.swapaxes(expert_ids[0], 0, 1)), keep(jnp.swapaxes(gate_scores[0], 0, 1)),
        keep(w_gate), keep(w_up), keep(w_down),
    )
    return pl.pallas_call(
        write,
        out_shape=shapes,
        in_specs=[vmem] * 4,
        out_specs=(far,) * 4,
        scratch_shapes=[dma((4,))],
        compiler_params=pltpu.CompilerParams(vmem_limit_bytes=16 * 2**20),
    )(*made)


def solution(mesh):
    return jax.shard_map(
        local,
        mesh=mesh,
        in_specs=(
            P("dp", "expert", None),
            P("dp", "expert", None),
            P("dp", None, None),
            P("dp", None, None),
            P("expert", None, "dp"),
            P("expert", None, "dp"),
            P("expert", "dp", None),
        ),
        out_specs=(
            P("dp", "expert", None),
            P("expert", None, "dp"),
            P("expert", None, "dp"),
            P("expert", "dp", None),
        ),
        check_vma=False,
    )
```

```python
import jax
import jax.numpy as jnp
from jax import lax
from jax.experimental import pallas as pl
from jax.experimental.pallas import tpu as pltpu
from jax.sharding import PartitionSpec as P

MESH = pl.DeviceIdType.MESH
F32, BF16 = jnp.float32, jnp.bfloat16

NE = 8
NZ = 8
NY = 4
NG = NY * 2
CAP = 7
D = 2048
HD = D // 2
FS = 128
R = NG * CAP
B = 2 * R
Q = HD // 2
CUT = 64
NA = 2
V = Q // NA
NQ = 4
W = Q // NQ
NT = (((1,), (1,)), ((), ()))


def dot(a, b):
    return jnp.dot(a, b, preferred_element_type=F32)


def dot_nt(a, b):
    return lax.dot_general(a, b, NT, preferred_element_type=F32)


def iota(shape, dim):
    return lax.broadcasted_iota(jnp.int32, shape, dim)


def spread(rows, cols, r_dim):
    r = iota((rows, cols), r_dim)
    c = iota((rows, cols), 1 - r_dim)
    low = jnp.where(r < R, r, r - R)
    group = (low * 37) >> 8
    place = group * 9 + low + jnp.where(r < R, 0, 8)
    return jnp.where(place == c, 1.0, 0.0).astype(BF16)


def kernel(
    tok, cot, ids_in, scores_in, wg, wu, wd,
    o_tok, o_gg, o_gu, o_gd,
    ids, scores, gbuf, gf, pick, ybuf, blocks, wx, wy, wdv, wsib, stack, stack_h, ssib, part, sbuf, rbuf, ysend, yrecv, esend, erecv,
    load_sem, own_sem, ws_send, ws_recv, g_send, g_recv, y_send, y_recv, sib_send, sib_recv, ag_send, ag_recv,
    ss_send, ss_recv, rs_send, rs_recv, y2_send, y2_recv, e_send, e_recv,
):
    e = lax.axis_index("expert")
    d = lax.axis_index("dp")
    z = d // NG
    g = d - z * NG
    h = g % 2
    e_x = e // 2
    e_y = e - 2 * e_x
    across = e + 1 - 2 * e_y
    along = [lax.rem(e_x + i, NE // 2) * 2 + e_y for i in (1, 3, 2)]
    sib = (e, d + 1 - 2 * h)
    zp = (e, lax.rem(z + 1, NZ) * NG + g)
    zm = (e, lax.rem(z + NZ - 1, NZ) * NG + g)

    def wrap(k):
        return lax.rem(k + 2 * NZ, NZ)

    sent = []

    def send(src, dst, s_sem, r_sem, to):
        copy = pltpu.make_async_remote_copy(
            src_ref=src, dst_ref=dst, send_sem=s_sem, recv_sem=r_sem, device_id=to, device_id_type=MESH
        )
        copy.start()
        sent.append(copy)

    def arrived(dst, r_sem):
        pltpu.make_async_remote_copy(
            src_ref=dst, dst_ref=dst, send_sem=r_sem, recv_sem=r_sem, device_id=sib, device_id_type=MESH
        ).wait_recv()

    barrier = pltpu.get_barrier_semaphore()
    beyond = [k + 1 - 2 * e_y for k in along]
    near_by = [(k, d) for k in (across, *beyond, *along)]
    near_by += [(e, z * NG + lax.rem(g + i, NG)) for i in range(1, NG)] + [zp, zm]
    for to in near_by:
        pl.semaphore_signal(barrier, inc=1, device_id=to, device_id_type=MESH)

    own = [
        pltpu.make_async_copy(tok.at[0], gbuf.at[e, 0], own_sem.at[0]),
        pltpu.make_async_copy(cot.at[0], gbuf.at[e, 1], own_sem.at[1]),
        pltpu.make_async_copy(ids_in, ids, own_sem.at[2]),
        pltpu.make_async_copy(scores_in, scores, own_sem.at[3]),
    ]
    for copy in own:
        copy.start()
    load_wd = pltpu.make_async_copy(wd.at[0], wdv, load_sem.at[8])
    load_wd.start()
    loads = []
    for n, w in enumerate((wg, wu)):
        for q in range(4):
            at = q % 2 * 2 * FS + n * FS
            loads.append(
                pltpu.make_async_copy(
                    w.at[0, q * Q : (q + 1) * Q, :], wx.at[q // 2, :, at : at + FS], load_sem.at[n * 4 + q]
                )
            )
    for copy in loads:
        copy.start()

    for copy in own:
        copy.wait()
    pl.semaphore_wait(barrier, len(near_by))

    for a, peers in enumerate(((*beyond, across, *along), (across, *along))):
        for i, k in enumerate(peers):
            send(gbuf.at[e, a], gbuf.at[e, a], g_send.at[a, i], g_recv.at[a, e], (k, d))
    for n, w in enumerate((wg, wu)):
        for f in range(2):
            rows = pl.ds(pl.multiple_of((1 - h) * HD + f * Q, Q), Q)
            send(w.at[0, rows, :], wsib.at[f, :, n * FS : (n + 1) * FS], ws_send.at[n, f], ws_recv.at[n, f], sib)

    hits = jnp.where(ids[...] == e, 1.0, 0.0)
    named_t = jnp.sum(hits, axis=0, keepdims=True)
    score_t = jnp.sum(hits * scores[...].astype(F32), axis=0, keepdims=True)
    row16, col16 = iota((16, 16), 0), iota((16, 16), 1)
    eye = jnp.where(row16 == col16, 1.0, 0.0)
    named = jnp.sum(eye * named_t, axis=1, keepdims=True)
    slot_t = jnp.sum(jnp.where(row16 < col16, named, 0.0), axis=0, keepdims=True)
    slot = jnp.sum(jnp.where(col16 < row16, named_t, 0.0), axis=1, keepdims=True)
    placing = jnp.where(slot_t == iota((8, 16), 0).astype(F32), named_t, 0.0)
    placing_t = jnp.where(slot == iota((16, 8), 1).astype(F32), named, 0.0)
    picking = (placing.astype(BF16), (placing * score_t).astype(BF16))
    gather = spread(B, NG * 16, 0)

    load_wd.wait()
    for q in range(4):
        wy[q // 2, :, q % 2 * FS : (q % 2 + 1) * FS] = wdv[:, q * Q : (q + 1) * Q].T

    arrived(gbuf.at[across, 0], g_recv.at[0, across])
    arrived(gbuf.at[across, 1], g_recv.at[1, across])
    for i, k in enumerate(along):
        send(gbuf.at[across, 1], gbuf.at[across, 1], g_send.at[1, 4 + i], g_recv.at[1, across], (k, d))

    for a in range(2):
        for k in along:
            for src in (k, k + 1 - 2 * e_y):
                arrived(gbuf.at[src, a], g_recv.at[a, src])
        for s in range(NE):
            gf[a, 2 * s : 2 * s + 2, :] = gbuf[s, a].astype(F32)
        picked = dot(picking[a], gf[a].astype(BF16))
        for c in range(2):
            at = c * HD
            both = jnp.concatenate([picked[:, at : at + Q], picked[:, at + Q : at + HD]], axis=0).astype(BF16)
            for n in range(NA):
                pick[a, n, c] = both[:, n * V : (n + 1) * V]
        for n in range(NA):
            for i in range(1, NG):
                to = lax.rem(g + i, NG)
                send(
                    pick.at[a, n, to % 2], ybuf.at[a, n, g], y_send.at[a, n, i], y_recv.at[a, n, g],
                    (e, z * NG + to),
                )
            ybuf[a, n, g] = pick[a, n, h]

    def ag_piece(a, k, c, n):
        return blocks.at[a, k, c, :, pl.ds(n * V, V)]

    def ag_start(way, step, a, k, n):
        ref = ag_piece(a, k, h, n)
        send(ref, ref, ag_send.at[way, step, a, n], ag_recv.at[way, step, a, n], (zp, zm)[way])

    def ag_wait(way, step, a, k, n):
        arrived(ag_piece(a, k, h, n), ag_recv.at[way, step, a, n])

    def to_sibling(a, k, n):
        ref = ag_piece(a, k, h, n)
        send(ref, ref, sib_send.at[a, k, n], sib_recv.at[a, k, n], sib)

    def fwd(k):
        for a in range(2):
            for n in range(NA):
                arrived(ag_piece(a, k, 1 - h, n), sib_recv.at[a, k, n])
        r = dot(blocks[0, k, 0], wx[0]) + dot(blocks[0, k, 1], wx[1])
        pre = r[:R, : 2 * FS] + r[R:, 2 * FS :]
        r = dot(blocks[1, k, 0], wy[0]) + dot(blocks[1, k, 1], wy[1])
        gh = r[:R, :FS] + r[R:, FS:]
        gate, up = pre[:, :FS], pre[:, FS:]
        sig = jax.nn.sigmoid(gate)
        act = gate * sig
        none = jnp.zeros((R, FS), F32)
        gate_delta = gh * up * sig * (1.0 + gate * (1.0 - sig))
        for n, delta in enumerate((gate_delta, gh * act)):
            stack[k, :, n * FS : (n + 1) * FS] = jnp.concatenate([delta, none], axis=0).astype(BF16)
            stack[k, :, (n + 2) * FS : (n + 3) * FS] = jnp.concatenate([none, delta], axis=0).astype(BF16)
        hidden = act * up
        stack_h[k, :, :FS] = jnp.concatenate([hidden, none], axis=0).astype(BF16)
        stack_h[k, :, FS:] = jnp.concatenate([none, hidden], axis=0).astype(BF16)
        send(stack.at[k, 0:CUT, 0 : 2 * FS], ssib.at[k], ss_send.at[k], ss_recv.at[k], sib)

    def row_grad(k):
        arrived(ssib.at[k], ss_recv.at[k])
        delta, delta_sib = stack[k, 0:CUT, 0 : 2 * FS], ssib[k]
        part[k] = jnp.concatenate(
            [
                (dot_nt(delta, wx[h, :, f * 2 * FS : (f + 1) * 2 * FS]) + dot_nt(delta_sib, wsib[f]))[:R]
                for f in range(2)
            ],
            axis=0,
        )

    for a in range(2):
        for n in range(NA):
            for i in range(1, NG):
                src = lax.rem(g + i, NG)
                arrived(ybuf.at[a, n, src], y_recv.at[a, n, src])
            blocks[a, z, h, :, n * V : (n + 1) * V] = dot(gather, ybuf[a, n].reshape(NG * 16, V)).astype(BF16)
            for way in range(2):
                ag_start(way, 0, a, z, n)
            to_sibling(a, z, n)
    for copy in loads:
        copy.wait()
    for n in range(2):
        for f in range(2):
            arrived(wsib.at[f, :, n * FS : (n + 1) * FS], ws_recv.at[n, f])

    def near(way, s):
        return wrap(z - s if way == 0 else z + s)

    def lanes(q):
        return pl.ds(q * W, W)

    def rs_start(way, step, q, value):
        sbuf[way, step, :, q * W : (q + 1) * W] = value.astype(BF16)
        send(
            sbuf.at[way, step, :, lanes(q)], rbuf.at[way, step, :, lanes(q)],
            rs_send.at[way, step, q], rs_recv.at[way, step, q], (zp, zm)[way],
        )

    def rs_take(way, step, q):
        arrived(rbuf.at[way, step, :, lanes(q)], rs_recv.at[way, step, q])
        return rbuf[way, step, :, q * W : (q + 1) * W].astype(F32)

    def part_of(k, q):
        return part[k, :, q * W : (q + 1) * W]

    work = {
        (1, 0): [(fwd, z)],
        (1, 1): [],
        (2, 0): [(fwd, near(0, 1)), (row_grad, z)],
        (2, 1): [(fwd, near(1, 1))],
        (3, 0): [(fwd, near(0, 2)), (row_grad, near(0, 1))],
        (3, 1): [(fwd, near(1, 2)), (row_grad, near(1, 1))],
    }
    for s in range(1, 4):
        for a in range(2):
            for n in range(NA):
                for way in range(2):
                    ag_wait(way, s - 1, a, near(way, s), n)
                    if s < 3 or a == way:
                        ag_start(way, s, a, near(way, s), n)
                    to_sibling(a, near(way, s), n)
            for f, k in work[s, a]:
                f(k)
    far = wrap(z + 4)
    fwd(near(0, 3))
    fwd(near(1, 3))
    for n in range(NA):
        for way in range(2):
            ag_wait(way, 3, way, far, n)
            to_sibling(way, far, n)
    for way in range(2):
        row_grad(near(way, 3))

    def first(way, q):
        return q % 2 == way

    for q in range(NQ):
        for way in range(2):
            if not first(way, q):
                rs_start(way, 1, q, part_of(near(1 - way, 3), q))
    fwd(far)
    row_grad(near(0, 2))
    row_grad(near(1, 2))
    row_grad(far)
    for q in range(NQ):
        for way in range(2):
            if first(way, q):
                rs_start(way, 0, q, part_of(far, q))

    def weight_grad(c):
        if c == 0:
            r = dot(stack_t, blocks[0, :, 0].reshape(NZ * B, Q))
        elif c == 1:
            r = dot(stack_t, blocks[0, :, 1].reshape(NZ * B, Q))
        else:
            r = None
        if r is not None:
            for f in range(2):
                at = c * HD + f * Q
                both = r[f * 2 * FS : (f + 1) * 2 * FS].T.astype(BF16)
                o_gg[0, at : at + Q, :] = both[:, :FS]
                o_gu[0, at : at + Q, :] = both[:, FS:]
            return
        stack_ht = stack_h[...].reshape(NZ * B, 2 * FS).T
        for c in range(2):
            r = dot(stack_ht, blocks[1, :, c].reshape(NZ * B, Q))
            for f in range(2):
                at = c * HD + f * Q
                o_gd[0, :, at : at + Q] = r[f * FS : (f + 1) * FS].astype(BF16)

    stack_t = stack[...].reshape(NZ * B, 4 * FS).T
    for j in range(1, 4):
        weight_grad(j - 1)
        for q in range(NQ):
            for way in range(2):
                if j == 1 and not first(way, q):
                    continue
                rs_start(way, j, q, part_of(near(1 - way, 4 - j), q) + rs_take(way, j - 1, q))

    scatter = spread(NG * 16, B, 1)
    for q in range(2):
        plane = jnp.concatenate(
            [
                (part_of(z, p) + rs_take(0, 3, p) + rs_take(1, 3, p)).astype(BF16)
                for p in range(q * NQ // 2, (q + 1) * NQ // 2)
            ],
            axis=1,
        )
        ysend[q] = dot(scatter, plane).astype(BF16).reshape(NG, 16, Q // 2)
        for i in range(1, NG):
            to = lax.rem(g + i, NG)
            send(ysend.at[q, to], yrecv.at[q, g], y2_send.at[q, i], y2_recv.at[q, g], (e, z * NG + to))
        yrecv[q, g] = ysend[q, g]
    early = len(sent)
    for q in range(2):
        for i in range(1, NG):
            src = lax.rem(g + i, NG)
            arrived(yrecv.at[q, src], y2_recv.at[q, src])
        rows = []
        for c in range(2):
            r = sum(yrecv[q, y * 2 + c].astype(F32) for y in range(NY))
            rows += [r[:8], r[8:]]
        rows = jnp.concatenate(rows, axis=1)
        total = placing_t[:, 0:1] * rows[0:1]
        for c in range(1, CAP):
            total += placing_t[:, c : c + 1] * rows[c : c + 1]
        for s in range(NE):
            esend[q, s] = total[2 * s : 2 * s + 2].astype(BF16)
        for i in range(1, NE):
            to = lax.rem(e + i, NE)
            send(esend.at[q, to], erecv.at[q, e], e_send.at[q, i], e_recv.at[q, e], (to, d))
        erecv[q, e] = esend[q, e]
    for copy in sent[:early]:
        copy.wait_send()
    for q in range(2):
        for i in range(1, NE):
            src = lax.rem(e + i, NE)
            arrived(erecv.at[q, src], e_recv.at[q, src])
        token = sum(erecv[q, s].astype(F32) for s in range(NE)).astype(BF16)
        for n in range(4):
            at = n * Q + q * (Q // 2)
            o_tok[0, :, at : at + Q // 2] = token[:, n * (Q // 2) : (n + 1) * (Q // 2)]
    for copy in sent[early:]:
        copy.wait_send()


def write(a0, a1, a2, a3, o0, o1, o2, o3, sems):
    copies = [
        pltpu.make_async_copy(src, dst, sems.at[i])
        for i, (src, dst) in enumerate(((a0, o0), (a1, o1), (a2, o2), (a3, o3)))
    ]
    for copy in copies:
        copy.start()
    for copy in copies:
        copy.wait()


def local(tokens, out_grad, expert_ids, gate_scores, w_gate, w_up, w_down):
    hbm = pl.BlockSpec(memory_space=pl.ANY)
    far = pl.BlockSpec(memory_space=pltpu.HBM)
    vmem = pl.BlockSpec(memory_space=pltpu.VMEM)
    dma = pltpu.SemaphoreType.DMA

    def keep(x):
        return pltpu.with_memory_space_constraint(x, pltpu.HBM)

    def like(x):
        return jax.ShapeDtypeStruct(x.shape, x.dtype)

    shapes = (like(tokens), like(w_gate), like(w_up), like(w_down))
    made = pl.pallas_call(
        kernel,
        out_shape=shapes,
        in_specs=[far] * 7,
        out_specs=(vmem,) * 4,
        scratch_shapes=[
            pltpu.VMEM((2, 16), jnp.int32),
            pltpu.VMEM((2, 16), BF16),
            pltpu.VMEM((NE, 2, 2, D), BF16),
            pltpu.VMEM((2, 16, D), F32),
            pltpu.VMEM((2, NA, 2, 16, V), BF16),
            pltpu.VMEM((2, NA, NG, 16, V), BF16),
            pltpu.VMEM((2, NZ, 2, B, Q), BF16),
            pltpu.VMEM((2, Q, 4 * FS), BF16),
            pltpu.VMEM((2, Q, 2 * FS), BF16),
            pltpu.VMEM((FS, D), BF16),
            pltpu.VMEM((2, Q, 2 * FS), BF16),
            pltpu.VMEM((NZ, B, 4 * FS), BF16),
            pltpu.VMEM((NZ, B, 2 * FS), BF16),
            pltpu.VMEM((NZ, CUT, 2 * FS), BF16),
            pltpu.VMEM((NZ, B, Q), F32),
            pltpu.VMEM((2, 4, B, Q), BF16),
            pltpu.VMEM((2, 4, B, Q), BF16),
            pltpu.VMEM((2, NG, 16, Q // 2), BF16),
            pltpu.VMEM((2, NG, 16, Q // 2), BF16),
            pltpu.VMEM((2, NE, 2, HD), BF16),
            pltpu.VMEM((2, NE, 2, HD), BF16),
            dma((9,)), dma((4,)), dma((2, 2)), dma((2, 2)),
            dma((2, 7)), dma((2, NE)), dma((2, NA, NG)), dma((2, NA, NG)),
            dma((2, NZ, NA)), dma((2, NZ, NA)), dma((2, 4, 2, NA)), dma((2, 4, 2, NA)),
            dma((NZ,)), dma((NZ,)), dma((2, 4, NQ)), dma((2, 4, NQ)),
            dma((2, NG)), dma((2, NG)), dma((2, NE)), dma((2, NE)),
        ],
        compiler_params=pltpu.CompilerParams(
            collective_id=0, has_side_effects=True, vmem_limit_bytes=40 * 2**20
        ),
        cost_estimate=pl.CostEstimate(flops=4 * 10**9, bytes_accessed=4 * 10**6, transcendentals=10**5),
    )(
        keep(tokens), keep(out_grad), keep(jnp.swapaxes(expert_ids[0], 0, 1)), keep(jnp.swapaxes(gate_scores[0], 0, 1)),
        keep(w_gate), keep(w_up), keep(w_down),
    )
    return pl.pallas_call(
        write,
        out_shape=shapes,
        in_specs=[vmem] * 4,
        out_specs=(far,) * 4,
        scratch_shapes=[dma((4,))],
        compiler_params=pltpu.CompilerParams(vmem_limit_bytes=16 * 2**20),
    )(*made)


def solution(mesh):
    return jax.shard_map(
        local,
        mesh=mesh,
        in_specs=(
            P("dp", "expert", None),
            P("dp", "expert", None),
            P("dp", None, None),
            P("dp", None, None),
            P("expert", None, "dp"),
            P("expert", None, "dp"),
            P("expert", "dp", None),
        ),
        out_specs=(
            P("dp", "expert", None),
            P("expert", None, "dp"),
            P("expert", None, "dp"),
            P("expert", "dp", None),
        ),
        check_vma=False,
    )
```
